128 devices in a mesh: row: 8 (over z, core), col: 16 (over y, x).
Axes of the slice: x: 4, y: 4, z: 4, core: 2. Of those that a mesh axis runs over, the one named last changes fastest.
Arguments:
- load_vectors: float32 [2, 64, 98304], P(None, 'col', 'row'), may hold values from -6 to 6
- panel_factor: float32 [2, 16, 8, 8, 98304], P(None, 'col', None, None, 'row'), may hold values from -0.125 to 0.125
- diag_inverse: float32 [2, 8, 128, 128], replicated, may hold values from -1.4 to 1.4
- trail_adjoint: float32 [2, 64, 97280], P(None, 'col', 'row'), may hold values from -0.615587 to 0.615587
- adjoint_loads: float32 [2, 64, 1024], replicated, may hold values from -6 to 6
Outputs:
- solution: float32 [2, 64, 1024], P(None, 'col')
- trail_residual: float32 [2, 64, 97280], P(None, 'col', 'row')
- adjoint_solution: float32 [2, 64, 1024], P(None, 'col')
The draws below stay inside these ranges and needn't reach their ends.
All inputs are finite; a program needn't handle non-finite values.
Results may differ from the reference program's by a relative error of at most 0.0001.
Values sent between devices are 32-bit elements; how exact they have to be, the bound alone decides.
No kernel may reach another device: no remote copies, remote signals or barrier semaphores. Data moves between devices by JAX's collectives and lax.ppermute only.
A program may use at most 128 MiB of HBM per device.

```python
import math
import jax
import jax.numpy as jnp
from jax import lax

NB = 128
STEPS = 8
NRHS = 64
RB_DEV = 96
CW = 8
ROWS = 98304
W = 1024
TRAIL = 97280
N_ROW = 8
N_COL = 16


def draw_diag_inverse(key, part):
    key = jax.random.fold_in(key, 7)
    key_off, key_mag, key_phase = jax.random.split(key, 3)
    identity = jnp.eye(NB, dtype=jnp.float32)
    offdiag = jax.random.normal(key_off, (2, STEPS, NB, NB), jnp.float32) * (0.35 / NB ** 0.5)
    offdiag = jnp.clip(offdiag, -1.0, 1.0)
    magnitude = jax.random.uniform(key_mag, (STEPS, NB), jnp.float32, 0.7, 1.4)
    phase = jax.random.uniform(key_phase, (STEPS, NB), jnp.float32, -math.pi, math.pi)
    diagonal = jnp.stack([magnitude * jnp.cos(phase), magnitude * jnp.sin(phase)])
    return offdiag * (1.0 - identity) + diagonal[..., None] * identity


def block_scale(rng, extent, cuts, low, largest):
    def one(dim, blocks):
        draws = jax.random.uniform(jax.random.fold_in(jax.random.fold_in(rng, 6), dim), (blocks,), jnp.float32, low / len(cuts), largest / len(cuts))
        return jnp.repeat(jnp.exp(draws), extent[dim] // blocks).reshape((-1,) + (1,) * (len(extent) - dim - 1))

    level = one(*cuts[0])
    for cut in cuts[1:]:
        level = level * one(*cut)
    return level


def centred(rng, shape, width, limit, cuts=(), held_as=jnp.bfloat16):
    entries = width * jax.random.normal(rng, shape, jnp.float32)
    if cuts:
        entries = entries * block_scale(rng, shape, cuts, -0.22, 0.18)
    return jnp.clip(entries, -limit, limit).astype(held_as)


def setup_inputs(seed: int = 0) -> dict:
    key_of = jax.random.split(jax.random.key(seed), 6)
    return {
        "load_vectors": centred(key_of[0], (2, NRHS, ROWS), 1.0, 6.0, ((1, 16), (2, 8)), jnp.float32),
        "panel_factor": centred(key_of[1], (2, N_COL, STEPS, CW, ROWS), (2 * STEPS * NB) ** -0.5, 0.125, ((1, 16), (4, 8)), jnp.float32),
        "diag_inverse": draw_diag_inverse(jax.random.fold_in(key_of[5], 71), 0),
        "trail_adjoint": centred(key_of[3], (2, NRHS, TRAIL), ((W / TRAIL) ** 0.5), 0.615587, ((1, 16), (2, 8)), jnp.float32),
        "adjoint_loads": centred(key_of[4], (2, NRHS, W), 1.0, 6.0, (), jnp.float32),
    }


def complex_product(pattern, former, latter, conjugate=False):
    highest = lax.Precision.HIGHEST
    former_re = former[0]
    former_im = former[1]
    if conjugate:
        former_im = -former_im
    real_part = jnp.einsum(pattern, former_re, latter[0], precision=highest) - jnp.einsum(pattern, former_im, latter[1], precision=highest)
    imag_part = jnp.einsum(pattern, former_re, latter[1], precision=highest) + jnp.einsum(pattern, former_im, latter[0], precision=highest)
    return jnp.stack([real_part, imag_part])


def reference(load_vectors, panel_factor, diag_inverse, trail_adjoint, adjoint_loads):
    depth = STEPS // N_ROW
    ordered = jnp.transpose(panel_factor, (0, 2, 1, 3, 4)).reshape(2, STEPS, NB, N_ROW, RB_DEV, NB)
    panel_window = ordered[:, :, :, :, :depth].reshape(2, STEPS, NB, N_ROW * depth * NB)
    panel_trail = ordered[:, :, :, :, depth:].reshape(2, STEPS, NB, N_ROW * (RB_DEV - depth) * NB)
    loads = load_vectors.reshape(2, NRHS, N_ROW, RB_DEV, NB)
    accum = loads[:, :, :, :depth].reshape(2, NRHS, N_ROW * depth * NB)
    loads_trail = loads[:, :, :, depth:].reshape(2, NRHS, N_ROW * (RB_DEV - depth) * NB)
    grid = jnp.arange(depth, dtype=jnp.int32)[None, :] * N_ROW + jnp.arange(N_ROW, dtype=jnp.int32)[:, None]
    levels = jnp.broadcast_to(grid[:, :, None], (N_ROW, depth, NB)).reshape(N_ROW * depth * NB)
    forward_parts = []
    for step in range(STEPS):
        start = ((step % N_ROW) * depth + step // N_ROW) * NB
        residual_block = accum[:, :, start:start + NB]
        solved = complex_product("bl,jl->bj", residual_block, diag_inverse[:, step])
        forward_parts.append(solved)
        update = complex_product("bj,jr->br", solved, panel_window[:, step])
        accum = accum - update * (levels > step).astype(jnp.float32)
    stacked = jnp.stack(forward_parts, 2)
    trail_residual = loads_trail - complex_product("bkj,kjr->br", stacked, panel_trail)
    zsums = complex_product("kjr,br->bkj", panel_trail, trail_adjoint, True)
    adjoint_window = jnp.zeros((2, NRHS, N_ROW * depth * NB), jnp.float32)
    adjoint_parts = [None] * STEPS
    for step in reversed(range(STEPS)):
        start = ((step % N_ROW) * depth + step // N_ROW) * NB
        masked = adjoint_window * (levels > step).astype(jnp.float32)
        summed = zsums[:, :, step] + complex_product("jr,br->bj", panel_window[:, step], masked, True)
        vector = adjoint_loads[:, :, step * NB:(step + 1) * NB] - summed
        solved = complex_product("lj,bl->bj", diag_inverse[:, step], vector, True)
        adjoint_window = lax.dynamic_update_slice(adjoint_window, solved, (0, 0, start))
        adjoint_parts[step] = solved
    solution = stacked.reshape(2, NRHS, STEPS * NB)
    adjoint_solution = jnp.stack(adjoint_parts, 2).reshape(2, NRHS, STEPS * NB)
    return solution, trail_residual, adjoint_solution
```

```python
import jax
import jax.numpy as jnp
from jax import lax
from jax.experimental import pallas as pl
from jax.experimental.pallas import tpu as pltpu
from jax.sharding import PartitionSpec as P

NB = 128
STEPS = 8
ROWS_AXIS = 8
COLS_AXIS = 16
PER_COL = 4
WIDTH = 8
LOCAL = 12288
TRAIL_LOCAL = 12160
TILE = 2432
F32 = jnp.float32
BF16 = jnp.bfloat16


def times_i(x):
    rows = x.shape[0]
    rolled = pltpu.roll(x.reshape(rows // 8, 8, x.shape[1]), 4, 1).reshape(x.shape)
    part = lax.broadcasted_iota(jnp.int32, x.shape, 0) % 8
    return jnp.where(part < 4, -rolled, rolled)


def dot_nn(a, b, precision=lax.Precision.HIGHEST):
    return lax.dot_general(a, b, (((1,), (0,)), ((), ())), precision=precision, preferred_element_type=F32)


def dot_nt(a, b, precision=lax.Precision.HIGHEST):
    return lax.dot_general(a, b, (((1,), (1,)), ((), ())), precision=precision, preferred_element_type=F32)


def split(x):
    high = x.astype(BF16)
    return high, (x - high.astype(F32)).astype(BF16)


def dot_split(dot, a, b):
    a_high, a_low = a
    b_high, b_low = b
    native = lax.Precision.DEFAULT
    return dot(a_high, b_high, native) + (dot(a_high, b_low, native) + dot(a_low, b_high, native))


def block_of(g_ref, row, step, part):
    first = part * (STEPS * WIDTH) + step * WIDTH
    return g_ref[row, :, first : first + WIDTH, :].reshape(NB, NB)


def forward_kernel(col_ref, g_ref, d_ref, own_ref, sol_ref, acc, xs):
    col = col_ref[0]
    loads = 2 * STEPS * WIDTH
    for row in range(STEPS):
        acc[row] = g_ref[row, :, loads : loads + 2 * PER_COL, :].reshape(NB, NB)
    lane = lax.broadcasted_iota(jnp.int32, (NB, NB), 1)
    own = jnp.zeros((NB, NB), F32)
    for step in range(STEPS):
        a = acc[step]
        left = jnp.concatenate([a, times_i(a)], axis=1)
        inverse = jnp.concatenate([d_ref[0, step], d_ref[1, step]], axis=1)
        x = dot_nt(left, inverse)
        ix = times_i(x)
        xs[step] = x
        left = jnp.concatenate([x, ix], axis=1)
        for row in range(step + 1, STEPS):
            right = jnp.concatenate([block_of(g_ref, row, step, 0), block_of(g_ref, row, step, 1)], axis=0)
            acc[row] -= dot_nn(left, right)
        mine = pltpu.roll(x, (step * WIDTH - col * WIDTH + NB) % NB, 1)
        mine_i = pltpu.roll(ix, (64 + step * WIDTH - col * WIDTH + NB) % NB, 1)
        own = jnp.where(lane // WIDTH == step, mine, own)
        own = jnp.where(lane // WIDTH == step + STEPS, mine_i, own)
        sol_ref[:, step * NB : (step + 1) * NB] = xs[step, pl.ds(pl.multiple_of(col * 8, 8), 8), :]
    own_ref[...] = own


def backward_kernel(v_ref, g_ref, d_ref, out_ref, acc):
    acc[...] = v_ref[...]
    for step in reversed(range(STEPS)):
        v = acc[step]
        right = jnp.concatenate([d_ref[0, step], -d_ref[1, step]], axis=0)
        y = dot_nn(jnp.concatenate([v, times_i(v)], axis=1), right)
        out_ref[:, step * NB : (step + 1) * NB] = y
        left = jnp.concatenate([y, times_i(y)], axis=1)
        for other in range(step):
            right = jnp.concatenate([block_of(g_ref, step, other, 0), -block_of(g_ref, step, other, 1)], axis=1)
            acc[other] -= dot_nt(left, right)


def trail_kernel(x_ref, l_ref, out_ref):
    out_ref[...] = -dot_split(dot_nn, split(x_ref[...]), split(l_ref[...]))


def zsum_kernel(ta_ref, l_ref, out_ref):
    @pl.when(pl.program_id(0) == 0)
    def _():
        out_ref[...] = jnp.zeros_like(out_ref)

    out_ref[...] += dot_split(dot_nt, split(ta_ref[...]), split(l_ref[...]))

    @pl.when(pl.program_id(0) == pl.num_programs(0) - 1)
    def _():
        q = out_ref[...]
        out_ref[...] = q - times_i(pltpu.roll(q, 64, 1))


FACTOR_SPEC = pl.BlockSpec((pl.Element(NB), pl.Element(TILE)), lambda i: (0, (i * (TILE // NB) + 1) * NB))
VMEM = pl.BlockSpec(memory_space=pltpu.VMEM)
SMEM = pl.BlockSpec(memory_space=pltpu.SMEM)


def body(load_vectors, panel_factor, diag_inverse, trail_adjoint, adjoint_loads):
    col = lax.axis_index("col")
    factor = panel_factor.reshape(NB, LOCAL)
    loads = load_vectors.reshape(2 * PER_COL, LOCAL)
    packed = jnp.concatenate([factor[:, :NB], loads[:, :NB]], axis=0)
    window = lax.all_gather(packed, ("row", "col")).reshape(ROWS_AXIS, COLS_AXIS, 136, NB)
    own, sol = pl.pallas_call(
        forward_kernel,
        out_shape=[jax.ShapeDtypeStruct((NB, NB), F32), jax.ShapeDtypeStruct((8, STEPS * NB), F32)],
        in_specs=[SMEM, VMEM, VMEM],
        out_specs=[VMEM, VMEM],
        scratch_shapes=[pltpu.VMEM((STEPS, NB, NB), F32), pltpu.VMEM((STEPS, NB, NB), F32)],
        compiler_params=pltpu.CompilerParams(vmem_limit_bytes=32 * 2**20),
        name="forward",
    )(col.reshape(1), window, diag_inverse)
    trail = pl.pallas_call(
        trail_kernel,
        out_shape=jax.ShapeDtypeStruct((NB, TRAIL_LOCAL), F32),
        grid=(TRAIL_LOCAL // TILE,),
        in_specs=[pl.BlockSpec((NB, NB), lambda i: (0, 0)), FACTOR_SPEC],
        out_specs=pl.BlockSpec((NB, TILE), lambda i: (0, i)),
        compiler_params=pltpu.CompilerParams(vmem_limit_bytes=32 * 2**20),
        name="trail",
    )(own, factor)
    gathered = lax.all_gather(trail_adjoint.reshape(8, TRAIL_LOCAL), "col", axis=0, tiled=True)
    zpart = pl.pallas_call(
        zsum_kernel,
        out_shape=jax.ShapeDtypeStruct((NB, NB), F32),
        grid=(TRAIL_LOCAL // TILE,),
        in_specs=[pl.BlockSpec((NB, TILE), lambda i: (0, i)), FACTOR_SPEC],
        out_specs=pl.BlockSpec((NB, NB), lambda i: (0, 0)),
        compiler_params=pltpu.CompilerParams(vmem_limit_bytes=32 * 2**20),
        name="zsum",
    )(gathered, factor)
    spread = jnp.broadcast_to(zpart[:, :64].reshape(1, COLS_AXIS, 8, 64), (ROWS_AXIS, COLS_AXIS, 8, 64))
    met = lax.all_to_all(spread.reshape(128, 8, 64), ("row", "col"), 0, 0)
    zsum = met.reshape(ROWS_AXIS, COLS_AXIS, 8, STEPS, WIDTH).sum(0).transpose(2, 1, 0, 3).reshape(STEPS, 8, NB)
    mine = lax.dynamic_slice_in_dim(adjoint_loads, col * PER_COL, PER_COL, 1)
    vector = mine.reshape(8, STEPS, NB).transpose(1, 0, 2) - zsum
    adj = pl.pallas_call(
        backward_kernel,
        out_shape=jax.ShapeDtypeStruct((8, STEPS * NB), F32),
        in_specs=[VMEM, VMEM, VMEM],
        out_specs=VMEM,
        scratch_shapes=[pltpu.VMEM((STEPS, 8, NB), F32)],
        compiler_params=pltpu.CompilerParams(vmem_limit_bytes=32 * 2**20),
        name="backward",
    )(vector, window, diag_inverse)
    mine_trail = lax.psum_scatter(trail.reshape(COLS_AXIS, 8, TRAIL_LOCAL), "col", scatter_dimension=0, tiled=False)
    residual = mine_trail.reshape(2, PER_COL, TRAIL_LOCAL) + load_vectors[:, :, NB:]
    return sol.reshape(2, PER_COL, STEPS * NB), residual, adj.reshape(2, PER_COL, STEPS * NB)


def solution(mesh):
    in_specs = (
        P(None, "col", "row"),
        P(None, "col", None, None, "row"),
        P(),
        P(None, "col", "row"),
        P(),
    )
    out_specs = (P(None, "col", None), P(None, "col", "row"), P(None, "col", None))
    return jax.shard_map(body, mesh=mesh, in_specs=in_specs, out_specs=out_specs, check_vma=False)
```

```python
import functools

import jax
import jax.numpy as jnp
from jax import lax
from jax.experimental import pallas as pl
from jax.experimental.pallas import tpu as pltpu
from jax.sharding import PartitionSpec as P

NB = 128
STEPS = 8
ROWS_AXIS = 8
COLS_AXIS = 16
PER_COL = 4
WIDTH = 8
LOCAL = 12288
TRAIL_LOCAL = 12160
SIDE = 4
TILES = 32
QUARTER = 1536
QTILES = QUARTER // NB
FIRST = (0, TRAIL_LOCAL - SIDE * QUARTER)
LIMIT = 8 * 2**20
MESSAGE = TILES // 2 + QTILES
F32 = jnp.float32
BF16 = jnp.bfloat16


def times_i(x):
    rows = x.shape[0]
    rolled = pltpu.roll(x.reshape(rows // 8, 8, x.shape[1]), 4, 1).reshape(x.shape)
    part = lax.broadcasted_iota(jnp.int32, x.shape, 0) % 8
    return jnp.where(part < 4, -rolled, rolled)


def dot_nn(a, b, precision=lax.Precision.HIGHEST):
    return lax.dot_general(a, b, (((1,), (0,)), ((), ())), precision=precision, preferred_element_type=F32)


def dot_nt(a, b, precision=lax.Precision.HIGHEST):
    return lax.dot_general(a, b, (((1,), (1,)), ((), ())), precision=precision, preferred_element_type=F32)


def split(x):
    high = x.astype(BF16)
    return high, (x - high.astype(F32)).astype(BF16)


def dot_split(dot, a, b):
    a_high, a_low = a
    b_high, b_low = b
    native = lax.Precision.DEFAULT
    return dot(a_high, b_high, native) + (dot(a_high, b_low, native) + dot(a_low, b_high, native))


def aligned(index, by):
    return pl.multiple_of(index, by)


def cut_kernel(distances, place_ref, f_ref, *refs):
    outs, sems = refs[-2 * len(distances) - 1 : -1], refs[-1]
    copies = []
    for half in range(2):
        for by in distances:
            i = len(copies)
            quarter = (place_ref[2 + half] + by) % SIDE
            first = aligned(NB + FIRST[half] + quarter * QUARTER, NB)
            copies.append(pltpu.make_async_copy(f_ref.at[:, pl.ds(first, QUARTER)], outs[i], sems.at[i]))
    for copy in copies:
        copy.start()
    for copy in copies:
        copy.wait()


def pack_kernel(place_ref, own_ref, one_ref, two_ref, three_ref, ta_ref, *refs):
    outs = refs[-2 * SIDE :]
    z, core = place_ref[0], place_ref[1]
    slabs = (own_ref, one_ref, two_ref, three_ref)

    def pick(chip, first):
        back = (z - chip + SIDE) % SIDE
        value = slabs[0][pl.ds(first, 8), :]
        for s in range(1, SIDE):
            value = jnp.where(back == s, slabs[s][pl.ds(first, 8), :], value)
        return value

    tiles = []
    for row in range(STEPS):
        other = jnp.where(core == row % 2, 0, 1)
        for step in range(row):
            tiles.append(pick(row // 2, aligned(other * (STEPS * WIDTH) + step * WIDTH, 8)))
    for chip in range(SIDE):
        tiles.append(pick(chip, 2 * STEPS * WIDTH))
    for half in range(2):
        for by in range(SIDE):
            out = outs[half * SIDE + by]
            for tile in range(TILES // 2):
                out[tile] = tiles[half * (TILES // 2) + tile]
            quarter = (place_ref[2 + half] + by) % SIDE
            for tile in range(QTILES):
                first = aligned(FIRST[half] + quarter * QUARTER + tile * NB, NB)
                value = ta_ref[:, pl.ds(first, NB)]
                if half == 1 and tile == 0:
                    value = jnp.where(quarter == 0, 0.0, value)
                out[TILES // 2 + tile] = value


def line_kernel(*refs):
    for half in range(2):
        for by in range(SIDE):
            refs[-2 + half][by] = refs[half * SIDE + by][...]


def repack_kernel(*refs):
    first, second, (blocks, ta_first, ta_second) = refs[:4], refs[4:8], refs[-3:]
    for dy in range(SIDE):
        for dx in range(SIDE):
            at = dy * SIDE + dx
            for half, (source, ta) in enumerate(((first[dx].at[dy], ta_first), (second[dy].at[dx], ta_second))):
                for tile in range(TILES // 2):
                    blocks[half * (TILES // 2) + tile, at] = source[tile]
                for tile in range(QTILES):
                    ta[at * 8 : at * 8 + 8, tile * NB : (tile + 1) * NB] = source[TILES // 2 + tile]


def either(core, which, mine_ref, other_ref, tile):
    return jnp.where(core == which, mine_ref[tile], other_ref[tile]).reshape(NB, NB)


def block_of(core, mine_ref, other_ref, row, step, part):
    return either(core, part, mine_ref, other_ref, row * (row - 1) // 2 + step)


def near_inverse(place_ref, d_ref, part, step):
    y, x = place_ref[2], place_ref[3]
    rows = []
    for dy in range(SIDE):
        for dx in range(SIDE):
            col = ((y - dy + SIDE) % SIDE) * SIDE + (x - dx + SIDE) % SIDE
            rows.append(d_ref[part, step, pl.ds(aligned(col * 8, 8), 8), :])
    return jnp.concatenate(rows, axis=0)


def store_parts(ref, step, value):
    for part in range(2):
        ref[part, :, step * NB : (step + 1) * NB] = value[part * PER_COL : (part + 1) * PER_COL]


def forward_kernel(place_ref, mine_ref, other_ref, d_ref, *refs):
    first_ref, second_ref, sol_ref, acc, own = refs[-5:]
    core = place_ref[1]
    for row in range(STEPS):
        acc[row] = either(core, row % 2, mine_ref, other_ref, 28 + row // 2)
    lane = lax.broadcasted_iota(jnp.int32, (NB, NB), 1)
    for step in range(STEPS):
        a = acc[step]
        left = jnp.concatenate([a, times_i(a)], axis=1)
        near = jnp.concatenate([near_inverse(place_ref, d_ref, part, step) for part in range(2)], axis=1)
        x = dot_nt(left, near)
        ix = times_i(x)
        natural = jnp.concatenate([d_ref[0, step], d_ref[1, step]], axis=1)
        store_parts(sol_ref, step, dot_nt(left[:8], natural))
        left = jnp.concatenate([x, ix], axis=1)
        for row in range(step + 1, STEPS):
            right = jnp.concatenate([block_of(core, mine_ref, other_ref, row, step, part) for part in range(2)], axis=0)
            acc[row] -= dot_nn(left, right)
        for half, apart in enumerate((SIDE * WIDTH, WIDTH)):
            for by in range(SIDE):
                at = half * SIDE + by
                mine = own[at] if step else jnp.zeros((NB, NB), F32)
                for part, value in enumerate((x, ix)):
                    to = part * STEPS + step
                    moved = pltpu.roll(value, (to * WIDTH - by * apart) % NB, 1)
                    mine = jnp.where(lane // WIDTH == to, moved, mine)
                own[at] = mine
    for by in range(SIDE):
        second_ref[:, by * NB : (by + 1) * NB] = own[SIDE + by]
        for dy in range(SIDE):
            for dx in range(SIDE):
                from_row, to_row = (dy * SIDE + dx) * 8, (dx * SIDE + dy) * 8
                first_ref[to_row : to_row + 8, by * NB : (by + 1) * NB] = own[by, from_row : from_row + 8]


def backward_kernel(place_ref, loads_ref, *refs):
    sums, (mine_ref, other_ref, d_ref, out_ref, acc) = refs[:4], refs[4:]
    core = place_ref[1]
    acc[...] = jnp.zeros_like(acc)
    for step in reversed(range(STEPS)):
        v = loads_ref[:, step * NB : (step + 1) * NB]
        v -= (sums[0][step] + sums[1][step]) + (sums[2][step] + sums[3][step])
        right = jnp.concatenate([d_ref[0, step], -d_ref[1, step]], axis=0)
        y = dot_nn(jnp.concatenate([v, times_i(v)], axis=1), right)
        if step < STEPS - 1:
            u = acc[step]
            near = [near_inverse(place_ref, d_ref, part, step) for part in range(2)]
            y -= dot_nn(jnp.concatenate([u, times_i(u)], axis=1), jnp.concatenate([near[0], -near[1]], axis=0))
        store_parts(out_ref, step, y)
        left = jnp.concatenate([y, times_i(y)], axis=1)
        for other in range(step):
            right = [block_of(core, mine_ref, other_ref, step, other, part) for part in range(2)]
            acc[other] += dot_nt(left, jnp.concatenate([right[0], -right[1]], axis=1))


def trail_kernel(*refs):
    outs = refs[-2 * SIDE :]
    for half in range(2):
        x_ref = refs[half]
        total = None
        for by in range(SIDE):
            piece = refs[2 + half * SIDE + by]
            term = dot_split(dot_nn, split(x_ref[:, by * NB : (by + 1) * NB]), split(piece[...]))
            total = term if total is None else total + term
        for by in range(SIDE):
            outs[half * SIDE + by][...] = -total[by * 32 : by * 32 + 32]


def zsum_kernel(place_ref, ta_first, ta_second, *refs):
    pieces, outs = refs[: 2 * SIDE], refs[-SIDE:]
    for half, ta_ref in enumerate((ta_first, ta_second)):
        ta = split(ta_ref[...])
        for by in range(SIDE):
            q = dot_split(dot_nt, ta, split(pieces[half * SIDE + by][...]))
            q = q - times_i(pltpu.roll(q, 64, 1))
            index = (place_ref[2 + half] - by + SIDE) % SIDE
            for dy in range(SIDE):
                part = q[dy * 32 : dy * 32 + 32, :64]
                outs[dy][index, :, half * 64 : half * 64 + 64] = part


def middle_kernel(place_ref, *refs):
    got, outs = refs[:SIDE], refs[-SIDE:]
    for dx in range(SIDE):
        rows = slice(dx * 8, dx * 8 + 8)
        for col in range(SIDE):
            values = [got[dy][col, rows, :] for dy in range(SIDE)]
            outs[dx][16 + col] = (values[0] + values[1]) + (values[2] + values[3])
            for dy in range(SIDE):
                outs[dx][((place_ref[2] + dy) % SIDE) * SIDE + col] = values[dy]


def last_kernel(place_ref, *refs):
    got, (out_ref, held) = refs[:SIDE], refs[SIDE:]
    for col in range(COLS_AXIS):
        value = (got[0][col] + got[1][col]) + (got[2][col] + got[3][col])
        held[col] = pltpu.roll(value, 64, 1)
    for dx in range(SIDE):
        for y in range(SIDE):
            held[y * SIDE + (place_ref[3] + dx) % SIDE] += got[dx][16 + y]
    lane = lax.broadcasted_iota(jnp.int32, (8, NB), 1)
    for step in range(STEPS):
        value = jnp.zeros((8, NB), F32)
        for col in range(COLS_AXIS):
            moved = pltpu.roll(held[col], ((col - step) * WIDTH) % NB, 1)
            value = jnp.where(lane // WIDTH == col, moved, value)
        out_ref[step] = value


def finish_kernel(place_ref, loads_ref, *refs):
    pieces, out_ref = refs[:-1], refs[-1]
    for half in range(2):
        for by in range(SIDE):
            quarter = (place_ref[2 + half] + by) % SIDE
            to = aligned(FIRST[half] + quarter * QUARTER, NB)
            value = pieces[half * SIDE + by][...]
            for part in range(2):
                rows = value[part * PER_COL : (part + 1) * PER_COL]
                loads = loads_ref[part, :, pl.ds(aligned(to + NB, NB), QUARTER)]
                out_ref[part, :, pl.ds(to, QUARTER)] = rows + loads


VMEM = pl.BlockSpec(memory_space=pltpu.VMEM)
SMEM = pl.BlockSpec(memory_space=pltpu.SMEM)
ANY = pl.BlockSpec(memory_space=pl.ANY)
HBM = pl.BlockSpec(memory_space=pltpu.HBM)


def call(kernel, name, shapes, args, scratch=(), after=(), far=(), us=1):
    specs = [SMEM if arg.dtype == jnp.int32 else VMEM for arg in args]
    specs = [HBM if i in far else spec for i, spec in enumerate(specs)] + [ANY] * len(after)
    args = [*args, *after]
    return pl.pallas_call(
        kernel,
        out_shape=[jax.ShapeDtypeStruct(shape, F32) for shape in shapes],
        in_specs=specs,
        out_specs=[VMEM] * len(shapes),
        scratch_shapes=list(scratch),
        compiler_params=pltpu.CompilerParams(vmem_limit_bytes=LIMIT),
        cost_estimate=pl.CostEstimate(flops=0, bytes_accessed=3_500_000 * us, transcendentals=0),
        name=name,
    )(*args)


def to_other_core(array):
    return lax.ppermute(array, "row", [(r, r ^ 1) for r in range(ROWS_AXIS)])


def up_z(array, by):
    return lax.ppermute(array, "row", [(r, (r + 2 * by) % ROWS_AXIS) for r in range(ROWS_AXIS)])


def up(array, axis, by):
    def moved(c):
        y, x = c // SIDE, c % SIDE
        return ((y + by) % SIDE) * SIDE + x if axis == "y" else y * SIDE + (x + by) % SIDE

    return lax.ppermute(array, "col", [(c, moved(c)) for c in range(COLS_AXIS)])


def to_all(pieces, axis, sign=1):
    return [pieces[0]] + [up(pieces[by], axis, sign * by) for by in (1, 2, 3)]


AXES = (("y", "x"), ("x", "y"))


def cut(place, factor, distances, after=()):
    return call(
        functools.partial(cut_kernel, distances),
        "cut",
        [(NB, QUARTER)] * 2 * len(distances),
        [place, factor],
        [pltpu.SemaphoreType.DMA((2 * len(distances),))],
        after,
        (1,),
    )


def body(load_vectors, panel_factor, diag_inverse, trail_adjoint, adjoint_loads):
    col, row = lax.axis_index("col"), lax.axis_index("row")
    place = jnp.stack([row // 2, row % 2, col // SIDE, col % SIDE]).astype(jnp.int32)
    core = row % 2
    factor = panel_factor.reshape(NB, LOCAL)
    parts = factor[:, :NB].reshape(2, STEPS * WIDTH, NB)
    keep = lax.dynamic_index_in_dim(parts, core, 0, False)
    got = to_other_core(lax.dynamic_index_in_dim(parts, 1 - core, 0, False))
    slab = jnp.concatenate([keep, got, load_vectors[:, :, :NB].reshape(8, NB)], axis=0)
    slabs = [slab] + [up_z(slab, by) for by in (1, 2, 3)]
    early = cut(place, factor, (1, 3))
    one = [up(early[2 * half], AXES[half][0], 1) for half in range(2)]
    three = [up(early[2 * half + 1], AXES[half][0], 3) for half in range(2)]
    messages = call(
        pack_kernel,
        "pack",
        [(MESSAGE, 8, NB)] * 8,
        [place, *slabs, trail_adjoint.reshape(8, TRAIL_LOCAL)],
        after=one + three,
    )
    heard = [to_all(messages[half * SIDE : half * SIDE + SIDE], AXES[half][0]) for half in range(2)]
    first_lines = call(line_kernel, "line", [(SIDE, MESSAGE, 8, NB)] * 2, heard[0] + heard[1])
    late = cut(place, factor, (0, 2), first_lines)
    two = [up(late[2 * half + 1], AXES[half][0], 2) for half in range(2)]
    pieces = [[late[2 * half], one[half], two[half], three[half]] for half in range(2)]
    lines = to_all([first_lines[0]] * SIDE, AXES[0][1]) + to_all([first_lines[1]] * SIDE, AXES[1][1])
    blocks, ta_first, ta_second = call(
        repack_kernel, "repack", [(TILES, COLS_AXIS, 8, NB)] + [(NB, QUARTER)] * 2, lines, after=two
    )
    window = (blocks, to_other_core(blocks))
    zparts = call(
        zsum_kernel,
        "zsum",
        [(SIDE, 32, NB)] * SIDE,
        [place, ta_first, ta_second, *pieces[0], *pieces[1]],
        us=3,
    )
    *trail_x, sol = call(
        forward_kernel,
        "forward",
        [(NB, SIDE * NB)] * 2 + [(2, PER_COL, STEPS * NB)],
        [place, *window, diag_inverse],
        [pltpu.VMEM((STEPS, NB, NB), F32)] * 2,
        after=[zparts[0]],
        us=6,
    )
    trail = call(trail_kernel, "trail", [(32, QUARTER)] * 2 * SIDE, [*trail_x, *pieces[0], *pieces[1]], us=3)
    zparts = call(middle_kernel, "middle", [(20, 8, NB)] * SIDE, [place, *to_all(zparts, "y", -1)], after=[trail[0]])
    (zown,) = call(
        last_kernel,
        "last",
        [(STEPS, 8, NB)],
        [place, *to_all(zparts, "x", -1)],
        [pltpu.VMEM((COLS_AXIS, 8, NB), F32)],
    )
    zchip = zown + to_other_core(zown)
    zsums = [zchip] + [up_z(zchip, by) for by in (1, 2, 3)]
    mine = lax.dynamic_slice_in_dim(adjoint_loads, col * PER_COL, PER_COL, 1).reshape(8, STEPS * NB)
    (adj,) = call(
        backward_kernel,
        "backward",
        [(2, PER_COL, STEPS * NB)],
        [place, mine, *zsums, *window, diag_inverse],
        [pltpu.VMEM((STEPS, 8, NB), F32)],
        us=6,
    )
    back = []
    for half in range(2):
        met = to_all(trail[half * SIDE : half * SIDE + SIDE], AXES[half][1], -1)
        total = (met[0] + met[1]) + (met[2] + met[3])
        back += to_all([total[by * 8 : by * 8 + 8] for by in range(SIDE)], AXES[half][0], -1)
    (residual,) = call(finish_kernel, "finish", [(2, PER_COL, TRAIL_LOCAL)], [place, load_vectors, *back])
    return sol, residual, adj


def solution(mesh):
    in_specs = (
        P(None, "col", "row"),
        P(None, "col", None, None, "row"),
        P(),
        P(None, "col", "row"),
        P(),
    )
    out_specs = (P(None, "col", None), P(None, "col", "row"), P(None, "col", None))
    return jax.shard_map(body, mesh=mesh, in_specs=in_specs, out_specs=out_specs, check_vma=False)
```

```python
import functools

import jax
import jax.numpy as jnp
from jax import lax
from jax.experimental import pallas as pl
from jax.experimental.pallas import tpu as pltpu
from jax.sharding import PartitionSpec as P

NB = 128
STEPS = 8
ROWS_AXIS = 8
COLS_AXIS = 16
PER_COL = 4
WIDTH = 8
LOCAL = 12288
TRAIL_LOCAL = 12160
SIDE = 4
TILES = 32
QUARTER = 1536
QTILES = QUARTER // NB
FIRST = (0, TRAIL_LOCAL - SIDE * QUARTER)
LIMIT = 8 * 2**20
MESSAGE = TILES // 2 + QTILES
F32 = jnp.float32
BF16 = jnp.bfloat16


def times_i(x):
    rows = x.shape[0]
    rolled = pltpu.roll(x.reshape(rows // 8, 8, x.shape[1]), 4, 1).reshape(x.shape)
    part = lax.broadcasted_iota(jnp.int32, x.shape, 0) % 8
    return jnp.where(part < 4, -rolled, rolled)


def dot_nn(a, b, precision):
    return lax.dot_general(a, b, (((1,), (0,)), ((), ())), precision=precision, preferred_element_type=F32)


def dot_nt(a, b, precision):
    return lax.dot_general(a, b, (((1,), (1,)), ((), ())), precision=precision, preferred_element_type=F32)


def split(x):
    high = x.astype(BF16)
    return high, (x - high.astype(F32)).astype(BF16)


def dot_split(dot, a, b):
    a_high, a_low = a
    b_high, b_low = b
    native = lax.Precision.DEFAULT
    return dot(a_high, b_high, native) + (dot(a_high, b_low, native) + dot(a_low, b_high, native))


def aligned(index, by):
    return pl.multiple_of(index, by)


def cut_kernel(distances, place_ref, f_ref, *refs):
    outs, sems = refs[-2 * len(distances) - 1 : -1], refs[-1]
    copies = []
    for half in range(2):
        for by in distances:
            i = len(copies)
            quarter = (place_ref[2 + half] + by) % SIDE
            first = aligned(NB + FIRST[half] + quarter * QUARTER, NB)
            copies.append(pltpu.make_async_copy(f_ref.at[:, pl.ds(first, QUARTER)], outs[i], sems.at[i]))
    for copy in copies:
        copy.start()
    for copy in copies:
        copy.wait()


def pack_kernel(place_ref, own_ref, one_ref, two_ref, three_ref, ta_ref, *refs):
    outs = refs[-2 * SIDE :]
    z, core = place_ref[0], place_ref[1]
    slabs = (own_ref, one_ref, two_ref, three_ref)

    def pick(chip, first):
        back = (z - chip + SIDE) % SIDE
        value = slabs[0][pl.ds(first, 8), :]
        for s in range(1, SIDE):
            value = jnp.where(back == s, slabs[s][pl.ds(first, 8), :], value)
        return value

    tiles = []
    for row in range(STEPS):
        other = jnp.where(core == row % 2, 0, 1)
        for step in range(row):
            tiles.append(pick(row // 2, aligned(other * (STEPS * WIDTH) + step * WIDTH, 8)))
    for chip in range(SIDE):
        tiles.append(pick(chip, 2 * STEPS * WIDTH))
    for half in range(2):
        for by in range(SIDE):
            out = outs[half * SIDE + by]
            for tile in range(TILES // 2):
                out[tile] = tiles[half * (TILES // 2) + tile]
            quarter = (place_ref[2 + half] + by) % SIDE
            for tile in range(QTILES):
                first = aligned(FIRST[half] + quarter * QUARTER + tile * NB, NB)
                value = ta_ref[:, pl.ds(first, NB)]
                if half == 1 and tile == 0:
                    value = jnp.where(quarter == 0, 0.0, value)
                out[TILES // 2 + tile] = value


def line_kernel(*refs):
    for half in range(2):
        for by in range(SIDE):
            refs[-2 + half][by] = refs[half * SIDE + by][...]


def repack_kernel(*refs):
    first, second, (blocks, ta_first, ta_second) = refs[:4], refs[4:8], refs[-3:]
    for dy in range(SIDE):
        for dx in range(SIDE):
            at = dy * SIDE + dx
            for half, (source, ta) in enumerate(((first[dx].at[dy], ta_first), (second[dy].at[dx], ta_second))):
                for tile in range(TILES // 2):
                    blocks[half * (TILES // 2) + tile, at] = source[tile]
                for tile in range(QTILES):
                    ta[at * 8 : at * 8 + 8, tile * NB : (tile + 1) * NB] = source[TILES // 2 + tile]


def either(core, which, mine_ref, other_ref, tile):
    return jnp.where(core == which, mine_ref[tile], other_ref[tile]).reshape(NB, NB)


def block_of(core, mine_ref, other_ref, row, step, part):
    return either(core, part, mine_ref, other_ref, row * (row - 1) // 2 + step)


def near_inverse(place_ref, d_ref, part, step):
    y, x = place_ref[2], place_ref[3]
    rows = []
    for dy in range(SIDE):
        for dx in range(SIDE):
            col = ((y - dy + SIDE) % SIDE) * SIDE + (x - dx + SIDE) % SIDE
            rows.append(d_ref[part, step, pl.ds(aligned(col * 8, 8), 8), :])
    return jnp.concatenate(rows, axis=0)


def store_parts(ref, step, value):
    for part in range(2):
        ref[part, :, step * NB : (step + 1) * NB] = value[part * PER_COL : (part + 1) * PER_COL]


def forward_kernel(place_ref, mine_ref, other_ref, d_ref, *refs):
    first_ref, second_ref, sol_ref, acc, own = refs[-5:]
    core = place_ref[1]
    for row in range(STEPS):
        acc[row] = either(core, row % 2, mine_ref, other_ref, 28 + row // 2)
    lane = lax.broadcasted_iota(jnp.int32, (NB, NB), 1)
    for step in range(STEPS):
        a = acc[step]
        left = split(jnp.concatenate([a, times_i(a)], axis=1))
        near = jnp.concatenate([near_inverse(place_ref, d_ref, part, step) for part in range(2)], axis=1)
        x = dot_split(dot_nt, left, split(near))
        ix = times_i(x)
        natural = jnp.concatenate([d_ref[0, step], d_ref[1, step]], axis=1)
        own_left = split(jnp.concatenate([a[:8], times_i(a[:8])], axis=1))
        store_parts(sol_ref, step, dot_split(dot_nt, own_left, split(natural)))
        left = split(jnp.concatenate([x, ix], axis=1))
        for row in range(step + 1, STEPS):
            right = jnp.concatenate([block_of(core, mine_ref, other_ref, row, step, part) for part in range(2)], axis=0)
            acc[row] -= dot_split(dot_nn, left, split(right))
        for half, apart in enumerate((SIDE * WIDTH, WIDTH)):
            for by in range(SIDE):
                at = half * SIDE + by
                mine = own[at] if step else jnp.zeros((NB, NB), F32)
                for part, value in enumerate((x, ix)):
                    to = part * STEPS + step
                    moved = pltpu.roll(value, (to * WIDTH - by * apart) % NB, 1)
                    mine = jnp.where(lane // WIDTH == to, moved, mine)
                own[at] = mine
    for by in range(SIDE):
        second_ref[:, by * NB : (by + 1) * NB] = own[SIDE + by]
        for dy in range(SIDE):
            for dx in range(SIDE):
                from_row, to_row = (dy * SIDE + dx) * 8, (dx * SIDE + dy) * 8
                first_ref[to_row : to_row + 8, by * NB : (by + 1) * NB] = own[by, from_row : from_row + 8]


def backward_kernel(place_ref, loads_ref, *refs):
    sums, (mine_ref, other_ref, d_ref, out_ref, acc) = refs[:4], refs[4:]
    core = place_ref[1]
    acc[...] = jnp.zeros_like(acc)
    for step in reversed(range(STEPS)):
        v = loads_ref[:, step * NB : (step + 1) * NB]
        v -= (sums[0][step] + sums[1][step]) + (sums[2][step] + sums[3][step])
        right = jnp.concatenate([d_ref[0, step], -d_ref[1, step]], axis=0)
        y = dot_split(dot_nn, split(jnp.concatenate([v, times_i(v)], axis=1)), split(right))
        if step < STEPS - 1:
            u = acc[step]
            near = [near_inverse(place_ref, d_ref, part, step) for part in range(2)]
            right = split(jnp.concatenate([near[0], -near[1]], axis=0))
            y -= dot_split(dot_nn, split(jnp.concatenate([u, times_i(u)], axis=1)), right)
        store_parts(out_ref, step, y)
        left = split(jnp.concatenate([y, times_i(y)], axis=1))
        for other in range(step):
            right = [block_of(core, mine_ref, other_ref, step, other, part) for part in range(2)]
            acc[other] += dot_split(dot_nt, left, split(jnp.concatenate([right[0], -right[1]], axis=1)))


def trail_term(x_ref, by, piece_ref):
    return dot_split(dot_nn, split(x_ref[:, by * NB : (by + 1) * NB]), split(piece_ref[...]))


def zsum_term(place_ref, ta, half, by, piece_ref, out):
    q = dot_split(dot_nt, ta, split(piece_ref[...]))
    q = q - times_i(pltpu.roll(q, 64, 1))
    index = (place_ref[2 + half] - by + SIDE) % SIDE
    for dy in range(SIDE):
        out[dy, index, :, half * 64 : half * 64 + 64] = q[dy * 32 : dy * 32 + 32, :64]


def early_kernel(place_ref, *refs):
    zout, touts = refs[-3], refs[-2:]
    for half in range(2):
        ta = split(refs[2 + half][...])
        total = None
        for i, by in enumerate((0, 1, 3)):
            piece = refs[4 + half * 3 + i]
            zsum_term(place_ref, ta, half, by, piece, zout)
            term = trail_term(refs[half], by, piece)
            total = term if total is None else total + term
        touts[half][...] = total


def late_kernel(place_ref, *refs):
    zin, tins, pieces, outs = refs[4], refs[5:7], refs[7:9], refs[-2 * SIDE - 1 : -1]
    zsums = refs[-1]
    zsums[...] = zin[...]
    for half in range(2):
        zsum_term(place_ref, split(refs[2 + half][...]), half, 2, pieces[half], zsums)
        total = tins[half][...] + trail_term(refs[half], 2, pieces[half])
        for by in range(SIDE):
            outs[half * SIDE + by][:, :QUARTER] = -total[by * 32 : by * 32 + 32]
    for dy in range(SIDE):
        for index in range(SIDE):
            outs[SIDE + dy][:, QUARTER + index * NB : QUARTER + (index + 1) * NB] = zsums[dy, index]


def middle_kernel(*refs):
    got, outs = (refs[:SIDE], refs[SIDE : 2 * SIDE]), refs[-2 * SIDE :]
    for by in range(SIDE):
        rows = slice(by * 8, by * 8 + 8)
        for half in range(2):
            values = [ref[rows, :QUARTER] for ref in got[half]]
            outs[half * SIDE + by][:, :QUARTER] = (values[0] + values[1]) + (values[2] + values[3])
        for col in range(SIDE):
            values = [ref[rows, QUARTER + col * NB : QUARTER + (col + 1) * NB] for ref in got[1]]
            values.append((values[0] + values[1]) + (values[2] + values[3]))
            for dy in range(SIDE + 1):
                to = QUARTER + (dy * SIDE + col) * NB
                outs[SIDE + by][:, to : to + NB] = values[dy]


def last_kernel(place_ref, *refs):
    got, (out_ref, held) = refs[:SIDE], refs[-2:]
    for dy in range(SIDE):
        for col in range(SIDE):
            at = QUARTER + (dy * SIDE + col) * NB
            values = [ref[:, at : at + NB] for ref in got]
            value = (values[0] + values[1]) + (values[2] + values[3])
            held[(place_ref[2] + dy) % SIDE * SIDE + col] = pltpu.roll(value, 64, 1)
    for dx in range(SIDE):
        for y in range(SIDE):
            at = QUARTER + (SIDE * SIDE + y) * NB
            held[y * SIDE + (place_ref[3] + dx) % SIDE] += got[dx][:, at : at + NB]
    lane = lax.broadcasted_iota(jnp.int32, (8, NB), 1)
    for step in range(STEPS):
        value = jnp.zeros((8, NB), F32)
        for col in range(COLS_AXIS):
            moved = pltpu.roll(held[col], ((col - step) * WIDTH) % NB, 1)
            value = jnp.where(lane // WIDTH == col, moved, value)
        out_ref[step] = value


def finish_kernel(place_ref, loads_ref, *refs):
    pieces, out_ref = refs[: 2 * SIDE], refs[-1]
    for half in range(2):
        for by in range(SIDE):
            quarter = (place_ref[2 + half] + by) % SIDE
            to = aligned(FIRST[half] + quarter * QUARTER, NB)
            value = pieces[half * SIDE + by][:, :QUARTER]
            for part in range(2):
                rows = value[part * PER_COL : (part + 1) * PER_COL]
                loads = loads_ref[part, :, pl.ds(aligned(to + NB, NB), QUARTER)]
                out_ref[part, :, pl.ds(to, QUARTER)] = rows + loads


VMEM = pl.BlockSpec(memory_space=pltpu.VMEM)
SMEM = pl.BlockSpec(memory_space=pltpu.SMEM)
ANY = pl.BlockSpec(memory_space=pl.ANY)
HBM = pl.BlockSpec(memory_space=pltpu.HBM)


def call(kernel, name, shapes, args, scratch=(), after=(), far=(), us=1):
    specs = [SMEM if arg.dtype == jnp.int32 else VMEM for arg in args]
    specs = [HBM if i in far else spec for i, spec in enumerate(specs)] + [ANY] * len(after)
    args = [*args, *after]
    return pl.pallas_call(
        kernel,
        out_shape=[jax.ShapeDtypeStruct(shape, F32) for shape in shapes],
        in_specs=specs,
        out_specs=[VMEM] * len(shapes),
        scratch_shapes=list(scratch),
        compiler_params=pltpu.CompilerParams(vmem_limit_bytes=LIMIT),
        cost_estimate=pl.CostEstimate(flops=0, bytes_accessed=3_500_000 * us, transcendentals=0),
        name=name,
    )(*args)


def to_other_core(array):
    return lax.ppermute(array, "row", [(r, r ^ 1) for r in range(ROWS_AXIS)])


def up_z(array, by):
    return lax.ppermute(array, "row", [(r, (r + 2 * by) % ROWS_AXIS) for r in range(ROWS_AXIS)])


def up(array, axis, by):
    def moved(c):
        y, x = c // SIDE, c % SIDE
        return ((y + by) % SIDE) * SIDE + x if axis == "y" else y * SIDE + (x + by) % SIDE

    return lax.ppermute(array, "col", [(c, moved(c)) for c in range(COLS_AXIS)])


def to_all(pieces, axis, sign=1):
    return [pieces[0]] + [up(pieces[by], axis, sign * by) for by in (1, 2, 3)]


AXES = (("y", "x"), ("x", "y"))


def cut(place, factor, distances, after=()):
    return call(
        functools.partial(cut_kernel, distances),
        "cut",
        [(NB, QUARTER)] * 2 * len(distances),
        [place, factor],
        [pltpu.SemaphoreType.DMA((2 * len(distances),))],
        after,
        (1,),
    )


def quarter_of(factor, place, half, by):
    return lax.dynamic_slice(factor, (0, NB + FIRST[half] + (place[2 + half] + by) % SIDE * QUARTER), (NB, QUARTER))


def body(load_vectors, panel_factor, diag_inverse, trail_adjoint, adjoint_loads):
    col, row = lax.axis_index("col"), lax.axis_index("row")
    place = jnp.stack([row // 2, row % 2, col // SIDE, col % SIDE]).astype(jnp.int32)
    core = row % 2
    factor = panel_factor.reshape(NB, LOCAL)
    parts = factor[:, :NB].reshape(2, STEPS * WIDTH, NB)
    keep = lax.dynamic_index_in_dim(parts, core, 0, False)
    got = to_other_core(lax.dynamic_index_in_dim(parts, 1 - core, 0, False))
    slab = jnp.concatenate([keep, got, load_vectors[:, :, :NB].reshape(8, NB)], axis=0)
    slabs = [slab] + [up_z(slab, by) for by in (1, 2, 3)]
    early = [quarter_of(factor, place, half, by) for half in range(2) for by in (1, 3)]
    one = [up(early[2 * half], AXES[half][0], 1) for half in range(2)]
    three = [up(early[2 * half + 1], AXES[half][0], 3) for half in range(2)]
    messages = call(
        pack_kernel,
        "pack",
        [(MESSAGE, 8, NB)] * 8,
        [place, *slabs, trail_adjoint.reshape(8, TRAIL_LOCAL)],
        after=one + three,
    )
    heard = [to_all(messages[half * SIDE : half * SIDE + SIDE], AXES[half][0]) for half in range(2)]
    first_lines = call(line_kernel, "line", [(SIDE, MESSAGE, 8, NB)] * 2, heard[0] + heard[1])
    lines = to_all([first_lines[0]] * SIDE, AXES[0][1]) + to_all([first_lines[1]] * SIDE, AXES[1][1])
    late = cut(place, factor, (0, 2), [lines[1], lines[5]])
    two = [up(late[2 * half + 1], AXES[half][0], 2) for half in range(2)]
    pieces = [[late[2 * half], one[half], two[half], three[half]] for half in range(2)]
    blocks, ta_first, ta_second = call(
        repack_kernel, "repack", [(TILES, COLS_AXIS, 8, NB)] + [(NB, QUARTER)] * 2, lines
    )
    window = (blocks, to_other_core(blocks))
    *trail_x, sol = call(
        forward_kernel,
        "forward",
        [(NB, SIDE * NB)] * 2 + [(2, PER_COL, STEPS * NB)],
        [place, *window, diag_inverse],
        [pltpu.VMEM((STEPS, NB, NB), F32)] * 2,
        us=6,
    )
    zpart, *tparts = call(
        early_kernel,
        "early",
        [(SIDE, SIDE, 32, NB)] + [(NB, QUARTER)] * 2,
        [place, *trail_x, ta_first, ta_second] + [pieces[half][by] for half in range(2) for by in (0, 1, 3)],
        us=6,
    )
    sent = call(
        late_kernel,
        "late",
        [(32, QUARTER)] * SIDE + [(32, QUARTER + SIDE * NB)] * SIDE,
        [place, *trail_x, ta_first, ta_second, zpart, *tparts, pieces[0][2], pieces[1][2]],
        [pltpu.VMEM((SIDE, SIDE, 32, NB), F32)],
        us=3,
    )
    met = [to_all(sent[half * SIDE : half * SIDE + SIDE], AXES[half][1], -1) for half in range(2)]
    sent = call(
        middle_kernel,
        "middle",
        [(8, QUARTER)] * SIDE + [(8, QUARTER + 20 * NB)] * SIDE,
        met[0] + met[1],
    )
    met = [to_all(sent[half * SIDE : half * SIDE + SIDE], AXES[half][0], -1) for half in range(2)]
    (zown,) = call(
        last_kernel, "last", [(STEPS, 8, NB)], [place, *met[1]], [pltpu.VMEM((COLS_AXIS, 8, NB), F32)]
    )
    zchip = zown + to_other_core(zown)
    zsums = [zchip] + [up_z(zchip, by) for by in (1, 2, 3)]
    mine = lax.dynamic_slice_in_dim(adjoint_loads, col * PER_COL, PER_COL, 1).reshape(8, STEPS * NB)
    (adj,) = call(
        backward_kernel,
        "backward",
        [(2, PER_COL, STEPS * NB)],
        [place, mine, *zsums, *window, diag_inverse],
        [pltpu.VMEM((STEPS, 8, NB), F32)],
        us=6,
    )
    (residual,) = call(
        finish_kernel,
        "finish",
        [(2, PER_COL, TRAIL_LOCAL)],
        [place, load_vectors, *met[0], *met[1]],
        after=[zown],
    )
    return sol, residual, adj


def solution(mesh):
    in_specs = (
        P(None, "col", "row"),
        P(None, "col", None, None, "row"),
        P(),
        P(None, "col", "row"),
        P(),
    )
    out_specs = (P(None, "col", None), P(None, "col", "row"), P(None, "col", None))
    return jax.shard_map(body, mesh=mesh, in_specs=in_specs, out_specs=out_specs, check_vma=False)
```

```python
import functools

import jax
import jax.numpy as jnp
from jax import lax
from jax.experimental import pallas as pl
from jax.experimental.pallas import tpu as pltpu
from jax.sharding import PartitionSpec as P

NB = 128
STEPS = 8
ROWS_AXIS = 8
COLS_AXIS = 16
PER_COL = 4
WIDTH = 8
LOCAL = 12288
TRAIL_LOCAL = 12160
SIDE = 4
TILES = 32
QUARTER = 1536
QTILES = QUARTER // NB
FIRST = (0, TRAIL_LOCAL - SIDE * QUARTER)
LIMIT = 8 * 2**20
MESSAGE = TILES // 2 + QTILES
F32 = jnp.float32
BF16 = jnp.bfloat16


def times_i(x):
    rows = x.shape[0]
    rolled = pltpu.roll(x.reshape(rows // 8, 8, x.shape[1]), 4, 1).reshape(x.shape)
    part = lax.broadcasted_iota(jnp.int32, x.shape, 0) % 8
    return jnp.where(part < 4, -rolled, rolled)


def dot_nn(a, b, precision):
    return lax.dot_general(a, b, (((1,), (0,)), ((), ())), precision=precision, preferred_element_type=F32)


def dot_nt(a, b, precision):
    return lax.dot_general(a, b, (((1,), (1,)), ((), ())), precision=precision, preferred_element_type=F32)


def split(x):
    high = x.astype(BF16)
    return high, (x - high.astype(F32)).astype(BF16)


def dot_split(dot, a, b):
    a_high, a_low = a
    b_high, b_low = b
    native = lax.Precision.DEFAULT
    return dot(a_high, b_high, native) + (dot(a_high, b_low, native) + dot(a_low, b_high, native))


def aligned(index, by):
    return pl.multiple_of(index, by)


def cut_kernel(distances, place_ref, f_ref, *refs):
    outs, sems = refs[-2 * len(distances) - 1 : -1], refs[-1]
    copies = []
    for half in range(2):
        for by in distances:
            i = len(copies)
            quarter = (place_ref[2 + half] + by) % SIDE
            first = aligned(NB + FIRST[half] + quarter * QUARTER, NB)
            copies.append(pltpu.make_async_copy(f_ref.at[:, pl.ds(first, QUARTER)], outs[i], sems.at[i]))
    for copy in copies:
        copy.start()
    for copy in copies:
        copy.wait()


def pack_kernel(place_ref, own_ref, one_ref, two_ref, three_ref, ta_ref, *refs):
    outs = refs[-2 * SIDE :]
    z, core = place_ref[0], place_ref[1]
    slabs = (own_ref, one_ref, two_ref, three_ref)

    def pick(chip, first):
        back = (z - chip + SIDE) % SIDE
        value = slabs[0][pl.ds(first, 8), :]
        for s in range(1, SIDE):
            value = jnp.where(back == s, slabs[s][pl.ds(first, 8), :], value)
        return value

    tiles = []
    for row in range(STEPS):
        other = jnp.where(core == row % 2, 0, 1)
        for step in range(row):
            tiles.append(pick(row // 2, aligned(other * (STEPS * WIDTH) + step * WIDTH, 8)))
    for chip in range(SIDE):
        tiles.append(pick(chip, 2 * STEPS * WIDTH))
    for half in range(2):
        for by in range(SIDE):
            out = outs[half * SIDE + by]
            for tile in range(TILES // 2):
                out[tile] = tiles[half * (TILES // 2) + tile]
            quarter = (place_ref[2 + half] + by) % SIDE
            for tile in range(QTILES):
                first = aligned(FIRST[half] + quarter * QUARTER + tile * NB, NB)
                value = ta_ref[:, pl.ds(first, NB)]
                if half == 1 and tile == 0:
                    value = jnp.where(quarter == 0, 0.0, value)
                out[TILES // 2 + tile] = value


def hold_kernel(*refs):
    ins, outs, sems = refs[:4], refs[-5:-1], refs[-1]
    copies = [pltpu.make_async_copy(ins[i], outs[i], sems.at[i]) for i in range(4)]
    for copy in copies:
        copy.start()
    for copy in copies:
        copy.wait()


def line_kernel(*refs):
    for half in range(2):
        for by in range(SIDE):
            refs[-2 + half][by] = refs[half * SIDE + by][...]


def repack_kernel(*refs):
    first, second, (blocks, ta_first, ta_second) = refs[:4], refs[4:8], refs[-3:]
    for dy in range(SIDE):
        for dx in range(SIDE):
            at = dy * SIDE + dx
            for half, (source, ta) in enumerate(((first[dx].at[dy], ta_first), (second[dy].at[dx], ta_second))):
                for tile in range(TILES // 2):
                    blocks[half * (TILES // 2) + tile, at] = source[tile]
                for tile in range(QTILES):
                    ta[at * 8 : at * 8 + 8, tile * NB : (tile + 1) * NB] = source[TILES // 2 + tile]


def either(core, which, mine_ref, other_ref, tile):
    return jnp.where(core == which, mine_ref[tile], other_ref[tile]).reshape(NB, NB)


def block_of(core, mine_ref, other_ref, row, step, part):
    return either(core, part, mine_ref, other_ref, row * (row - 1) // 2 + step)


def near_inverse(place_ref, d_ref, part, step):
    y, x = place_ref[2], place_ref[3]
    rows = []
    for dy in range(SIDE):
        for dx in range(SIDE):
            col = ((y - dy + SIDE) % SIDE) * SIDE + (x - dx + SIDE) % SIDE
            rows.append(d_ref[part, step, pl.ds(aligned(col * 8, 8), 8), :])
    return jnp.concatenate(rows, axis=0)


def store_parts(ref, step, value):
    for part in range(2):
        ref[part, :, step * NB : (step + 1) * NB] = value[part * PER_COL : (part + 1) * PER_COL]


def forward_kernel(place_ref, mine_ref, other_ref, d_ref, *refs):
    first_ref, second_ref, sol_ref, acc, own = refs[-5:]
    core = place_ref[1]
    for row in range(STEPS):
        acc[row] = either(core, row % 2, mine_ref, other_ref, 28 + row // 2)
    lane = lax.broadcasted_iota(jnp.int32, (NB, NB), 1)
    for step in range(STEPS):
        a = acc[step]
        left = split(jnp.concatenate([a, times_i(a)], axis=1))
        near = jnp.concatenate([near_inverse(place_ref, d_ref, part, step) for part in range(2)], axis=1)
        x = dot_split(dot_nt, left, split(near))
        ix = times_i(x)
        natural = jnp.concatenate([d_ref[0, step], d_ref[1, step]], axis=1)
        own_left = split(jnp.concatenate([a[:8], times_i(a[:8])], axis=1))
        store_parts(sol_ref, step, dot_split(dot_nt, own_left, split(natural)))
        left = split(jnp.concatenate([x, ix], axis=1))
        for row in range(step + 1, STEPS):
            right = jnp.concatenate([block_of(core, mine_ref, other_ref, row, step, part) for part in range(2)], axis=0)
            acc[row] -= dot_split(dot_nn, left, split(right))
        for half, apart in enumerate((SIDE * WIDTH, WIDTH)):
            for by in range(SIDE):
                at = half * SIDE + by
                mine = own[at] if step else jnp.zeros((NB, NB), F32)
                for part, value in enumerate((x, ix)):
                    to = part * STEPS + step
                    moved = pltpu.roll(value, (to * WIDTH - by * apart) % NB, 1)
                    mine = jnp.where(lane // WIDTH == to, moved, mine)
                own[at] = mine
    for by in range(SIDE):
        second_ref[:, by * NB : (by + 1) * NB] = own[SIDE + by]
        for dy in range(SIDE):
            for dx in range(SIDE):
                from_row, to_row = (dy * SIDE + dx) * 8, (dx * SIDE + dy) * 8
                first_ref[to_row : to_row + 8, by * NB : (by + 1) * NB] = own[by, from_row : from_row + 8]


def backward_kernel(place_ref, loads_ref, *refs):
    sums, (mine_ref, other_ref, d_ref, out_ref, acc) = refs[:4], refs[4:]
    core = place_ref[1]
    acc[...] = jnp.zeros_like(acc)
    for step in reversed(range(STEPS)):
        v = loads_ref[:, step * NB : (step + 1) * NB]
        v -= (sums[0][step] + sums[1][step]) + (sums[2][step] + sums[3][step])
        right = jnp.concatenate([d_ref[0, step], -d_ref[1, step]], axis=0)
        y = dot_split(dot_nn, split(jnp.concatenate([v, times_i(v)], axis=1)), split(right))
        if step < STEPS - 1:
            u = acc[step]
            near = [near_inverse(place_ref, d_ref, part, step) for part in range(2)]
            right = split(jnp.concatenate([near[0], -near[1]], axis=0))
            y -= dot_split(dot_nn, split(jnp.concatenate([u, times_i(u)], axis=1)), right)
        store_parts(out_ref, step, y)
        left = split(jnp.concatenate([y, times_i(y)], axis=1))
        for other in range(step):
            right = [block_of(core, mine_ref, other_ref, step, other, part) for part in range(2)]
            acc[other] += dot_split(dot_nt, left, split(jnp.concatenate([right[0], -right[1]], axis=1)))


def trail_term(x_ref, by, piece_ref):
    return dot_split(dot_nn, split(x_ref[:, by * NB : (by + 1) * NB]), split(piece_ref[...]))


def zsum_term(place_ref, ta, half, by, piece_ref, out):
    q = dot_split(dot_nt, ta, split(piece_ref[...]))
    q = q - times_i(pltpu.roll(q, 64, 1))
    index = (place_ref[2 + half] - by + SIDE) % SIDE
    for dy in range(SIDE):
        out[dy, index, :, half * 64 : half * 64 + 64] = q[dy * 32 : dy * 32 + 32, :64]


def early_kernel(place_ref, *refs):
    zout, touts = refs[-3], refs[-2:]
    for half in range(2):
        ta = split(refs[2 + half][...])
        total = None
        for i, by in enumerate((0, 1, 3)):
            piece = refs[4 + half * 3 + i]
            zsum_term(place_ref, ta, half, by, piece, zout)
            term = trail_term(refs[half], by, piece)
            total = term if total is None else total + term
        touts[half][...] = total


def late_kernel(place_ref, *refs):
    zin, tins, pieces, outs = refs[4], refs[5:7], refs[7:9], refs[-2 * SIDE - 1 : -1]
    zsums = refs[-1]
    zsums[...] = zin[...]
    for half in range(2):
        zsum_term(place_ref, split(refs[2 + half][...]), half, 2, pieces[half], zsums)
        total = tins[half][...] + trail_term(refs[half], 2, pieces[half])
        for by in range(SIDE):
            outs[half * SIDE + by][:, :QUARTER] = -total[by * 32 : by * 32 + 32]
    for dy in range(SIDE):
        for index in range(SIDE):
            outs[SIDE + dy][:, QUARTER + index * NB : QUARTER + (index + 1) * NB] = zsums[dy, index]


def middle_kernel(*refs):
    got, outs = (refs[:SIDE], refs[SIDE : 2 * SIDE]), refs[-2 * SIDE :]
    for by in range(SIDE):
        rows = slice(by * 8, by * 8 + 8)
        for half in range(2):
            values = [ref[rows, :QUARTER] for ref in got[half]]
            outs[half * SIDE + by][:, :QUARTER] = (values[0] + values[1]) + (values[2] + values[3])
        for col in range(SIDE):
            values = [ref[rows, QUARTER + col * NB : QUARTER + (col + 1) * NB] for ref in got[1]]
            values.append((values[0] + values[1]) + (values[2] + values[3]))
            for dy in range(SIDE + 1):
                to = QUARTER + (dy * SIDE + col) * NB
                outs[SIDE + by][:, to : to + NB] = values[dy]


def last_kernel(place_ref, *refs):
    got, (out_ref, held) = refs[:SIDE], refs[-2:]
    for dy in range(SIDE):
        for col in range(SIDE):
            at = QUARTER + (dy * SIDE + col) * NB
            values = [ref[:, at : at + NB] for ref in got]
            value = (values[0] + values[1]) + (values[2] + values[3])
            held[(place_ref[2] + dy) % SIDE * SIDE + col] = pltpu.roll(value, 64, 1)
    for dx in range(SIDE):
        for y in range(SIDE):
            at = QUARTER + (SIDE * SIDE + y) * NB
            held[y * SIDE + (place_ref[3] + dx) % SIDE] += got[dx][:, at : at + NB]
    lane = lax.broadcasted_iota(jnp.int32, (8, NB), 1)
    for step in range(STEPS):
        value = jnp.zeros((8, NB), F32)
        for col in range(COLS_AXIS):
            moved = pltpu.roll(held[col], ((col - step) * WIDTH) % NB, 1)
            value = jnp.where(lane // WIDTH == col, moved, value)
        out_ref[step] = value


def finish_kernel(place_ref, loads_ref, *refs):
    pieces, out_ref = refs[: 2 * SIDE], refs[-1]
    for half in range(2):
        for by in range(SIDE):
            quarter = (place_ref[2 + half] + by) % SIDE
            to = aligned(FIRST[half] + quarter * QUARTER, NB)
            value = pieces[half * SIDE + by][:, :QUARTER]
            for part in range(2):
                rows = value[part * PER_COL : (part + 1) * PER_COL]
                loads = loads_ref[part, :, pl.ds(aligned(to + NB, NB), QUARTER)]
                out_ref[part, :, pl.ds(to, QUARTER)] = rows + loads


VMEM = pl.BlockSpec(memory_space=pltpu.VMEM)
SMEM = pl.BlockSpec(memory_space=pltpu.SMEM)
ANY = pl.BlockSpec(memory_space=pl.ANY)


def call(kernel, name, shapes, args, scratch=(), after=(), far=(), us=1):
    specs = [SMEM if arg.dtype == jnp.int32 else VMEM for arg in args]
    specs = [ANY if i in far else spec for i, spec in enumerate(specs)] + [ANY] * len(after)
    args = [*args, *after]
    return pl.pallas_call(
        kernel,
        out_shape=[jax.ShapeDtypeStruct(shape, F32) for shape in shapes],
        in_specs=specs,
        out_specs=[VMEM] * len(shapes),
        scratch_shapes=list(scratch),
        compiler_params=pltpu.CompilerParams(vmem_limit_bytes=LIMIT),
        cost_estimate=pl.CostEstimate(flops=0, bytes_accessed=3_500_000 * us, transcendentals=0),
        name=name,
    )(*args)


def to_other_core(array):
    return lax.ppermute(array, "row", [(r, r ^ 1) for r in range(ROWS_AXIS)])


def up_z(array, by):
    return lax.ppermute(array, "row", [(r, (r + 2 * by) % ROWS_AXIS) for r in range(ROWS_AXIS)])


def up(array, axis, by):
    def moved(c):
        y, x = c // SIDE, c % SIDE
        return ((y + by) % SIDE) * SIDE + x if axis == "y" else y * SIDE + (x + by) % SIDE

    return lax.ppermute(array, "col", [(c, moved(c)) for c in range(COLS_AXIS)])


def to_all(pieces, axis, sign=1):
    return [pieces[0]] + [up(pieces[by], axis, sign * by) for by in (1, 2, 3)]


AXES = (("y", "x"), ("x", "y"))


def cut(place, factor, distances, after=()):
    return call(
        functools.partial(cut_kernel, distances),
        "cut",
        [(NB, QUARTER)] * 2 * len(distances),
        [place, factor],
        [pltpu.SemaphoreType.DMA((2 * len(distances),))],
        after,
        (1,),
    )


def quarter_of(factor, place, half, by):
    return lax.dynamic_slice(factor, (0, NB + FIRST[half] + (place[2 + half] + by) % SIDE * QUARTER), (NB, QUARTER))


def body(load_vectors, panel_factor, diag_inverse, trail_adjoint, adjoint_loads):
    col, row = lax.axis_index("col"), lax.axis_index("row")
    place = jnp.stack([row // 2, row % 2, col // SIDE, col % SIDE]).astype(jnp.int32)
    core = row % 2
    factor = panel_factor.reshape(NB, LOCAL)
    parts = factor[:, :NB].reshape(2, STEPS * WIDTH, NB)
    keep = lax.dynamic_index_in_dim(parts, core, 0, False)
    got = to_other_core(lax.dynamic_index_in_dim(parts, 1 - core, 0, False))
    slab = jnp.concatenate([keep, got, load_vectors[:, :, :NB].reshape(8, NB)], axis=0)
    slabs = [slab] + [up_z(slab, by) for by in (1, 2, 3)]
    early = [quarter_of(factor, place, half, by) for half in range(2) for by in (1, 3)]
    one = [up(early[2 * half], AXES[half][0], 1) for half in range(2)]
    three = [up(early[2 * half + 1], AXES[half][0], 3) for half in range(2)]
    messages = call(
        pack_kernel,
        "pack",
        [(MESSAGE, 8, NB)] * 8,
        [place, *slabs, trail_adjoint.reshape(8, TRAIL_LOCAL)],
        after=one + three,
    )
    heard = [to_all(messages[half * SIDE : half * SIDE + SIDE], AXES[half][0]) for half in range(2)]
    first_lines = call(line_kernel, "line", [(SIDE, MESSAGE, 8, NB)] * 2, heard[0] + heard[1])
    lines = to_all([first_lines[0]] * SIDE, AXES[0][1]) + to_all([first_lines[1]] * SIDE, AXES[1][1])
    late = cut(place, factor, (0, 2), [lines[1], lines[5]])
    two = [up(late[2 * half + 1], AXES[half][0], 2) for half in range(2)]
    pieces = [[late[2 * half], one[half], two[half], three[half]] for half in range(2)]
    blocks, ta_first, ta_second = call(
        repack_kernel, "repack", [(TILES, COLS_AXIS, 8, NB)] + [(NB, QUARTER)] * 2, lines
    )
    window = (blocks, to_other_core(blocks))
    *trail_x, sol = call(
        forward_kernel,
        "forward",
        [(NB, SIDE * NB)] * 2 + [(2, PER_COL, STEPS * NB)],
        [place, *window, diag_inverse],
        [pltpu.VMEM((STEPS, NB, NB), F32)] * 2,
        us=6,
    )
    zpart, *tparts = call(
        early_kernel,
        "early",
        [(SIDE, SIDE, 32, NB)] + [(NB, QUARTER)] * 2,
        [place, *trail_x, ta_first, ta_second] + [pieces[half][by] for half in range(2) for by in (0, 1, 3)],
        us=6,
    )
    sent = call(
        late_kernel,
        "late",
        [(32, QUARTER)] * SIDE + [(32, QUARTER + SIDE * NB)] * SIDE,
        [place, *trail_x, ta_first, ta_second, zpart, *tparts, pieces[0][2], pieces[1][2]],
        [pltpu.VMEM((SIDE, SIDE, 32, NB), F32)],
        us=3,
    )
    mine = lax.dynamic_slice_in_dim(adjoint_loads, col * PER_COL, PER_COL, 1).reshape(8, STEPS * NB)
    held = call(
        hold_kernel,
        "hold",
        [window[0].shape, window[1].shape, diag_inverse.shape, mine.shape],
        [*window, diag_inverse, mine],
        [pltpu.SemaphoreType.DMA((4,))],
        sent[:1],
        range(4),
    )
    met = [to_all(sent[half * SIDE : half * SIDE + SIDE], AXES[half][1], -1) for half in range(2)]
    sent = call(
        middle_kernel,
        "middle",
        [(8, QUARTER)] * SIDE + [(8, QUARTER + 20 * NB)] * SIDE,
        met[0] + met[1],
        after=held[:1],
    )
    met = [to_all(sent[half * SIDE : half * SIDE + SIDE], AXES[half][0], -1) for half in range(2)]
    (zown,) = call(
        last_kernel, "last", [(STEPS, 8, NB)], [place, *met[1]], [pltpu.VMEM((COLS_AXIS, 8, NB), F32)]
    )
    zchip = zown + to_other_core(zown)
    zsums = [zchip] + [up_z(zchip, by) for by in (1, 2, 3)]
    (adj,) = call(
        backward_kernel,
        "backward",
        [(2, PER_COL, STEPS * NB)],
        [place, held[3], *zsums, *held[:3]],
        [pltpu.VMEM((STEPS, 8, NB), F32)],
        us=6,
    )
    (residual,) = call(
        finish_kernel,
        "finish",
        [(2, PER_COL, TRAIL_LOCAL)],
        [place, load_vectors, *met[0], *met[1]],
        after=[zown],
    )
    return sol, residual, adj


def solution(mesh):
    in_specs = (
        P(None, "col", "row"),
        P(None, "col", None, None, "row"),
        P(),
        P(None, "col", "row"),
        P(),
    )
    out_specs = (P(None, "col", None), P(None, "col", "row"), P(None, "col", None))
    return jax.shard_map(body, mesh=mesh, in_specs=in_specs, out_specs=out_specs, check_vma=False)
```

```python
import functools

import jax
import jax.numpy as jnp
from jax import lax
from jax.experimental import pallas as pl
from jax.experimental.pallas import tpu as pltpu
from jax.sharding import PartitionSpec as P

NB = 128
STEPS = 8
ROWS_AXIS = 8
COLS_AXIS = 16
PER_COL = 4
WIDTH = 8
LOCAL = 12288
TRAIL_LOCAL = 12160
SIDE = 4
TILES = 32
QUARTER = 1536
QTILES = QUARTER // NB
FIRST = (0, TRAIL_LOCAL - SIDE * QUARTER)
LIMIT = 8 * 2**20
MESSAGE = TILES // 2 + QTILES
F32 = jnp.float32
BF16 = jnp.bfloat16


def times_i(x):
    rows = x.shape[0]
    rolled = pltpu.roll(x.reshape(rows // 8, 8, x.shape[1]), 4, 1).reshape(x.shape)
    part = lax.broadcasted_iota(jnp.int32, x.shape, 0) % 8
    return jnp.where(part < 4, -rolled, rolled)


def dot_nn(a, b, precision):
    return lax.dot_general(a, b, (((1,), (0,)), ((), ())), precision=precision, preferred_element_type=F32)


def dot_nt(a, b, precision):
    return lax.dot_general(a, b, (((1,), (1,)), ((), ())), precision=precision, preferred_element_type=F32)


def split(x):
    high = x.astype(BF16)
    return high, (x - high.astype(F32)).astype(BF16)


def dot_split(dot, a, b):
    a_high, a_low = a
    b_high, b_low = b
    native = lax.Precision.DEFAULT
    return dot(a_high, b_high, native) + (dot(a_high, b_low, native) + dot(a_low, b_high, native))


def aligned(index, by):
    return pl.multiple_of(index, by)


def cut_kernel(distances, place_ref, f_ref, *refs):
    outs, sems = refs[-2 * len(distances) - 1 : -1], refs[-1]
    copies = []
    for half in range(2):
        for by in distances:
            i = len(copies)
            quarter = (place_ref[2 + half] + by) % SIDE
            first = aligned(NB + FIRST[half] + quarter * QUARTER, NB)
            copies.append(pltpu.make_async_copy(f_ref.at[:, pl.ds(first, QUARTER)], outs[i], sems.at[i]))
    for copy in copies:
        copy.start()
    for copy in copies:
        copy.wait()


def pack_kernel(place_ref, own_ref, one_ref, two_ref, three_ref, ta_ref, *refs):
    outs = refs[-2 * SIDE :]
    z, core = place_ref[0], place_ref[1]
    slabs = (own_ref, one_ref, two_ref, three_ref)

    def pick(chip, first):
        back = (z - chip + SIDE) % SIDE
        value = slabs[0][pl.ds(first, 8), :]
        for s in range(1, SIDE):
            value = jnp.where(back == s, slabs[s][pl.ds(first, 8), :], value)
        return value

    tiles = []
    for row in range(STEPS):
        other = jnp.where(core == row % 2, 0, 1)
        for step in range(row):
            tiles.append(pick(row // 2, aligned(other * (STEPS * WIDTH) + step * WIDTH, 8)))
    for chip in range(SIDE):
        tiles.append(pick(chip, 2 * STEPS * WIDTH))
    for half in range(2):
        for by in range(SIDE):
            out = outs[half * SIDE + by]
            for tile in range(TILES // 2):
                out[tile] = tiles[half * (TILES // 2) + tile]
            quarter = (place_ref[2 + half] + by) % SIDE
            for tile in range(QTILES):
                first = aligned(FIRST[half] + quarter * QUARTER + tile * NB, NB)
                value = ta_ref[:, pl.ds(first, NB)]
                if half == 1 and tile == 0:
                    value = jnp.where(quarter == 0, 0.0, value)
                out[TILES // 2 + tile] = value


def hold_kernel(*refs):
    ins, outs, sems = refs[:4], refs[-5:-1], refs[-1]
    copies = [pltpu.make_async_copy(ins[i], outs[i], sems.at[i]) for i in range(4)]
    for copy in copies:
        copy.start()
    for copy in copies:
        copy.wait()


def line_kernel(*refs):
    for half in range(2):
        for by in range(SIDE):
            refs[-2 + half][by] = refs[half * SIDE + by][...]


def repack_kernel(*refs):
    first, second, (blocks, ta_first, ta_second) = refs[:4], refs[4:8], refs[-3:]
    for dy in range(SIDE):
        for dx in range(SIDE):
            at = dy * SIDE + dx
            for half, (source, ta) in enumerate(((first[dx].at[dy], ta_first), (second[dy].at[dx], ta_second))):
                for tile in range(TILES // 2):
                    blocks[half * (TILES // 2) + tile, at] = source[tile]
                for tile in range(QTILES):
                    ta[at * 8 : at * 8 + 8, tile * NB : (tile + 1) * NB] = source[TILES // 2 + tile]


def either(core, which, mine_ref, other_ref, tile):
    return jnp.where(core == which, mine_ref[tile], other_ref[tile]).reshape(NB, NB)


def block_of(core, mine_ref, other_ref, row, step, part):
    return either(core, part, mine_ref, other_ref, row * (row - 1) // 2 + step)


def near_inverse(place_ref, d_ref, part, step):
    y, x = place_ref[2], place_ref[3]
    rows = []
    for dy in range(SIDE):
        for dx in range(SIDE):
            col = ((y - dy + SIDE) % SIDE) * SIDE + (x - dx + SIDE) % SIDE
            rows.append(d_ref[part, step, pl.ds(aligned(col * 8, 8), 8), :])
    return jnp.concatenate(rows, axis=0)


def store_parts(ref, step, value):
    for part in range(2):
        ref[part, :, step * NB : (step + 1) * NB] = value[part * PER_COL : (part + 1) * PER_COL]


def forward_kernel(place_ref, mine_ref, other_ref, d_ref, *refs):
    first_ref, second_ref, sol_ref, acc, own = refs[-5:]
    core = place_ref[1]
    for row in range(STEPS):
        acc[row] = either(core, row % 2, mine_ref, other_ref, 28 + row // 2)
    lane = lax.broadcasted_iota(jnp.int32, (NB, NB), 1)
    for step in range(STEPS):
        a = acc[step]
        left = split(jnp.concatenate([a, times_i(a)], axis=1))
        near = jnp.concatenate([near_inverse(place_ref, d_ref, part, step) for part in range(2)], axis=1)
        x = dot_split(dot_nt, left, split(near))
        ix = times_i(x)
        natural = jnp.concatenate([d_ref[0, step], d_ref[1, step]], axis=1)
        own_left = split(jnp.concatenate([a[:8], times_i(a[:8])], axis=1))
        store_parts(sol_ref, step, dot_split(dot_nt, own_left, split(natural)))
        left = split(jnp.concatenate([x, ix], axis=1))
        for row in range(step + 1, STEPS):
            right = jnp.concatenate([block_of(core, mine_ref, other_ref, row, step, part) for part in range(2)], axis=0)
            acc[row] -= dot_split(dot_nn, left, split(right))
        for half, apart in enumerate((SIDE * WIDTH, WIDTH)):
            for by in range(SIDE):
                at = half * SIDE + by
                mine = own[at] if step else jnp.zeros((NB, NB), F32)
                for part, value in enumerate((x, ix)):
                    to = part * STEPS + step
                    moved = pltpu.roll(value, (to * WIDTH - by * apart) % NB, 1)
                    mine = jnp.where(lane // WIDTH == to, moved, mine)
                own[at] = mine
    for by in range(SIDE):
        second_ref[:, by * NB : (by + 1) * NB] = own[SIDE + by]
        for dy in range(SIDE):
            for dx in range(SIDE):
                from_row, to_row = (dy * SIDE + dx) * 8, (dx * SIDE + dy) * 8
                first_ref[to_row : to_row + 8, by * NB : (by + 1) * NB] = own[by, from_row : from_row + 8]


def backward_kernel(place_ref, loads_ref, *refs):
    sums, (mine_ref, other_ref, d_ref, out_ref, acc) = refs[:4], refs[4:]
    core = place_ref[1]
    acc[...] = jnp.zeros_like(acc)
    for step in reversed(range(STEPS)):
        v = loads_ref[:, step * NB : (step + 1) * NB]
        v -= (sums[0][step] + sums[1][step]) + (sums[2][step] + sums[3][step])
        right = jnp.concatenate([d_ref[0, step], -d_ref[1, step]], axis=0)
        y = dot_split(dot_nn, split(jnp.concatenate([v, times_i(v)], axis=1)), split(right))
        if step < STEPS - 1:
            u = acc[step]
            near = [near_inverse(place_ref, d_ref, part, step) for part in range(2)]
            right = split(jnp.concatenate([near[0], -near[1]], axis=0))
            y -= dot_split(dot_nn, split(jnp.concatenate([u, times_i(u)], axis=1)), right)
        store_parts(out_ref, step, y)
        left = split(jnp.concatenate([y, times_i(y)], axis=1))
        for other in range(step):
            right = [block_of(core, mine_ref, other_ref, step, other, part) for part in range(2)]
            acc[other] += dot_split(dot_nt, left, split(jnp.concatenate([right[0], -right[1]], axis=1)))


def trail_term(x_ref, by, piece_ref):
    return dot_split(dot_nn, split(x_ref[:, by * NB : (by + 1) * NB]), split(piece_ref[...]))


def zsum_term(place_ref, ta, half, by, piece_ref, out):
    q = dot_split(dot_nt, ta, split(piece_ref[...]))
    q = q - times_i(pltpu.roll(q, 64, 1))
    index = (place_ref[2 + half] - by + SIDE) % SIDE
    for dy in range(SIDE):
        out[dy, index, :, half * 64 : half * 64 + 64] = q[dy * 32 : dy * 32 + 32, :64]


def zsum_kernel(place_ref, *refs):
    for half in range(2):
        ta = split(refs[half][...])
        for by in range(SIDE):
            zsum_term(place_ref, ta, half, by, refs[2 + half * SIDE + by], refs[-1])


def trail_kernel(*refs):
    zsums, outs = refs[2], refs[-2 * SIDE :]
    for half in range(2):
        total = None
        for by in range(SIDE):
            term = trail_term(refs[half], by, refs[3 + half * SIDE + by])
            total = term if total is None else total + term
        for by in range(SIDE):
            outs[half * SIDE + by][:, :QUARTER] = -total[by * 32 : by * 32 + 32]
    for dy in range(SIDE):
        for index in range(SIDE):
            outs[SIDE + dy][:, QUARTER + index * NB : QUARTER + (index + 1) * NB] = zsums[dy, index]


def middle_kernel(*refs):
    got, outs = (refs[:SIDE], refs[SIDE : 2 * SIDE]), refs[-2 * SIDE :]
    for by in range(SIDE):
        rows = slice(by * 8, by * 8 + 8)
        for half in range(2):
            values = [ref[rows, :QUARTER] for ref in got[half]]
            outs[half * SIDE + by][:, :QUARTER] = (values[0] + values[1]) + (values[2] + values[3])
        for col in range(SIDE):
            values = [ref[rows, QUARTER + col * NB : QUARTER + (col + 1) * NB] for ref in got[1]]
            values.append((values[0] + values[1]) + (values[2] + values[3]))
            for dy in range(SIDE + 1):
                to = QUARTER + (dy * SIDE + col) * NB
                outs[SIDE + by][:, to : to + NB] = values[dy]


def last_kernel(place_ref, *refs):
    got, (out_ref, held) = refs[:SIDE], refs[-2:]
    for dy in range(SIDE):
        for col in range(SIDE):
            at = QUARTER + (dy * SIDE + col) * NB
            values = [ref[:, at : at + NB] for ref in got]
            value = (values[0] + values[1]) + (values[2] + values[3])
            held[(place_ref[2] + dy) % SIDE * SIDE + col] = pltpu.roll(value, 64, 1)
    for dx in range(SIDE):
        for y in range(SIDE):
            at = QUARTER + (SIDE * SIDE + y) * NB
            held[y * SIDE + (place_ref[3] + dx) % SIDE] += got[dx][:, at : at + NB]
    lane = lax.broadcasted_iota(jnp.int32, (8, NB), 1)
    for step in range(STEPS):
        value = jnp.zeros((8, NB), F32)
        for col in range(COLS_AXIS):
            moved = pltpu.roll(held[col], ((col - step) * WIDTH) % NB, 1)
            value = jnp.where(lane // WIDTH == col, moved, value)
        out_ref[step] = value


def finish_kernel(place_ref, loads_ref, *refs):
    pieces, out_ref = refs[: 2 * SIDE], refs[-1]
    for half in range(2):
        for by in range(SIDE):
            quarter = (place_ref[2 + half] + by) % SIDE
            to = aligned(FIRST[half] + quarter * QUARTER, NB)
            value = pieces[half * SIDE + by][:, :QUARTER]
            for part in range(2):
                rows = value[part * PER_COL : (part + 1) * PER_COL]
                loads = loads_ref[part, :, pl.ds(aligned(to + NB, NB), QUARTER)]
                out_ref[part, :, pl.ds(to, QUARTER)] = rows + loads


VMEM = pl.BlockSpec(memory_space=pltpu.VMEM)
SMEM = pl.BlockSpec(memory_space=pltpu.SMEM)
ANY = pl.BlockSpec(memory_space=pl.ANY)


def call(kernel, name, shapes, args, scratch=(), after=(), far=(), us=1):
    specs = [SMEM if arg.dtype == jnp.int32 else VMEM for arg in args]
    specs = [ANY if i in far else spec for i, spec in enumerate(specs)] + [ANY] * len(after)
    args = [*args, *after]
    return pl.pallas_call(
        kernel,
        out_shape=[jax.ShapeDtypeStruct(shape, F32) for shape in shapes],
        in_specs=specs,
        out_specs=[VMEM] * len(shapes),
        scratch_shapes=list(scratch),
        compiler_params=pltpu.CompilerParams(vmem_limit_bytes=LIMIT),
        cost_estimate=pl.CostEstimate(flops=0, bytes_accessed=3_500_000 * us, transcendentals=0),
        name=name,
    )(*args)


def to_other_core(array):
    return lax.ppermute(array, "row", [(r, r ^ 1) for r in range(ROWS_AXIS)])


def up_z(array, by):
    return lax.ppermute(array, "row", [(r, (r + 2 * by) % ROWS_AXIS) for r in range(ROWS_AXIS)])


def up(array, axis, by):
    def moved(c):
        y, x = c // SIDE, c % SIDE
        return ((y + by) % SIDE) * SIDE + x if axis == "y" else y * SIDE + (x + by) % SIDE

    return lax.ppermute(array, "col", [(c, moved(c)) for c in range(COLS_AXIS)])


def to_all(pieces, axis, sign=1):
    return [pieces[0]] + [up(pieces[by], axis, sign * by) for by in (1, 2, 3)]


AXES = (("y", "x"), ("x", "y"))


def cut(place, factor, distances, after=()):
    return call(
        functools.partial(cut_kernel, distances),
        "cut",
        [(NB, QUARTER)] * 2 * len(distances),
        [place, factor],
        [pltpu.SemaphoreType.DMA((2 * len(distances),))],
        after,
        (1,),
    )


def quarter_of(factor, place, half, by):
    return lax.dynamic_slice(factor, (0, NB + FIRST[half] + (place[2 + half] + by) % SIDE * QUARTER), (NB, QUARTER))


def body(load_vectors, panel_factor, diag_inverse, trail_adjoint, adjoint_loads):
    col, row = lax.axis_index("col"), lax.axis_index("row")
    place = jnp.stack([row // 2, row % 2, col // SIDE, col % SIDE]).astype(jnp.int32)
    core = row % 2
    factor = panel_factor.reshape(NB, LOCAL)
    parts = factor[:, :NB].reshape(2, STEPS * WIDTH, NB)
    keep = lax.dynamic_index_in_dim(parts, core, 0, False)
    got = to_other_core(lax.dynamic_index_in_dim(parts, 1 - core, 0, False))
    slab = jnp.concatenate([keep, got, load_vectors[:, :, :NB].reshape(8, NB)], axis=0)
    slabs = [slab] + [up_z(slab, by) for by in (1, 2, 3)]
    early = [quarter_of(factor, place, half, by) for half in range(2) for by in (1, 3)]
    one = [up(early[2 * half], AXES[half][0], 1) for half in range(2)]
    three = [up(early[2 * half + 1], AXES[half][0], 3) for half in range(2)]
    messages = call(
        pack_kernel,
        "pack",
        [(MESSAGE, 8, NB)] * 8,
        [place, *slabs, trail_adjoint.reshape(8, TRAIL_LOCAL)],
        after=one + three,
    )
    late = cut(place, factor, (0, 2), [early[0]])
    two = [up(late[2 * half + 1], AXES[half][0], 2) for half in range(2)]
    pieces = [[late[2 * half], one[half], two[half], three[half]] for half in range(2)]
    heard = [to_all(messages[half * SIDE : half * SIDE + SIDE], AXES[half][0]) for half in range(2)]
    first_lines = call(line_kernel, "line", [(SIDE, MESSAGE, 8, NB)] * 2, heard[0] + heard[1], after=two)
    lines = to_all([first_lines[0]] * SIDE, AXES[0][1]) + to_all([first_lines[1]] * SIDE, AXES[1][1])
    blocks, ta_first, ta_second = call(
        repack_kernel, "repack", [(TILES, COLS_AXIS, 8, NB)] + [(NB, QUARTER)] * 2, lines
    )
    window = (blocks, to_other_core(blocks))
    (zsums,) = call(
        zsum_kernel, "zsum", [(SIDE, SIDE, 32, NB)], [place, ta_first, ta_second, *pieces[0], *pieces[1]]
    )
    *trail_x, sol = call(
        forward_kernel,
        "forward",
        [(NB, SIDE * NB)] * 2 + [(2, PER_COL, STEPS * NB)],
        [place, *window, diag_inverse],
        [pltpu.VMEM((STEPS, NB, NB), F32)] * 2,
        after=[zsums],
        us=6,
    )
    sent = call(
        trail_kernel,
        "trail",
        [(32, QUARTER)] * SIDE + [(32, QUARTER + SIDE * NB)] * SIDE,
        [*trail_x, zsums, *pieces[0], *pieces[1]],
    )
    mine = lax.dynamic_slice_in_dim(adjoint_loads, col * PER_COL, PER_COL, 1).reshape(8, STEPS * NB)
    held = call(
        hold_kernel,
        "hold",
        [window[0].shape, window[1].shape, diag_inverse.shape, mine.shape],
        [*window, diag_inverse, mine],
        [pltpu.SemaphoreType.DMA((4,))],
        sent[:1],
        range(4),
    )
    met = [to_all(sent[half * SIDE : half * SIDE + SIDE], AXES[half][1], -1) for half in range(2)]
    sent = call(
        middle_kernel,
        "middle",
        [(8, QUARTER)] * SIDE + [(8, QUARTER + 20 * NB)] * SIDE,
        met[0] + met[1],
        after=held[:1],
    )
    met = [to_all(sent[half * SIDE : half * SIDE + SIDE], AXES[half][0], -1) for half in range(2)]
    (zown,) = call(
        last_kernel, "last", [(STEPS, 8, NB)], [place, *met[1]], [pltpu.VMEM((COLS_AXIS, 8, NB), F32)]
    )
    zchip = zown + to_other_core(zown)
    chips = [zchip] + [up_z(zchip, by) for by in (1, 2, 3)]
    (adj,) = call(
        backward_kernel,
        "backward",
        [(2, PER_COL, STEPS * NB)],
        [place, held[3], *chips, *held[:3]],
        [pltpu.VMEM((STEPS, 8, NB), F32)],
        us=6,
    )
    (residual,) = call(
        finish_kernel,
        "finish",
        [(2, PER_COL, TRAIL_LOCAL)],
        [place, load_vectors, *met[0], *met[1]],
        after=[zown],
    )
    return sol, residual, adj


def solution(mesh):
    in_specs = (
        P(None, "col", "row"),
        P(None, "col", None, None, "row"),
        P(),
        P(None, "col", "row"),
        P(),
    )
    out_specs = (P(None, "col", None), P(None, "col", "row"), P(None, "col", None))
    return jax.shard_map(body, mesh=mesh, in_specs=in_specs, out_specs=out_specs, check_vma=False)
```

```python
import functools

import jax
import jax.numpy as jnp
from jax import lax
from jax.experimental import pallas as pl
from jax.experimental.pallas import tpu as pltpu
from jax.sharding import PartitionSpec as P

NB = 128
STEPS = 8
ROWS_AXIS = 8
COLS_AXIS = 16
PER_COL = 4
WIDTH = 8
LOCAL = 12288
TRAIL_LOCAL = 12160
SIDE = 4
TILES = 32
QUARTER = 1536
QTILES = QUARTER // NB
FIRST = (0, TRAIL_LOCAL - SIDE * QUARTER)
LIMIT = 8 * 2**20
MESSAGE = TILES // 2 + QTILES
F32 = jnp.float32
BF16 = jnp.bfloat16


def times_i(x):
    rows = x.shape[0]
    rolled = pltpu.roll(x.reshape(rows // 8, 8, x.shape[1]), 4, 1).reshape(x.shape)
    part = lax.broadcasted_iota(jnp.int32, x.shape, 0) % 8
    return jnp.where(part < 4, -rolled, rolled)


def dot_nn(a, b, precision):
    return lax.dot_general(a, b, (((1,), (0,)), ((), ())), precision=precision, preferred_element_type=F32)


def dot_nt(a, b, precision):
    return lax.dot_general(a, b, (((1,), (1,)), ((), ())), precision=precision, preferred_element_type=F32)


def split(x):
    high = x.astype(BF16)
    return high, (x - high.astype(F32)).astype(BF16)


def dot_split(dot, a, b):
    a_high, a_low = a
    b_high, b_low = b
    native = lax.Precision.DEFAULT
    return dot(a_high, b_high, native) + (dot(a_high, b_low, native) + dot(a_low, b_high, native))


def aligned(index, by):
    return pl.multiple_of(index, by)


def cut_kernel(distances, place_ref, f_ref, *refs):
    outs, sems = refs[-2 * len(distances) - 1 : -1], refs[-1]
    copies = []
    for half in range(2):
        for by in distances:
            i = len(copies)
            quarter = (place_ref[2 + half] + by) % SIDE
            first = aligned(NB + FIRST[half] + quarter * QUARTER, NB)
            copies.append(pltpu.make_async_copy(f_ref.at[:, pl.ds(first, QUARTER)], outs[i], sems.at[i]))
    for copy in copies:
        copy.start()
    for copy in copies:
        copy.wait()


def pack_kernel(place_ref, own_ref, one_ref, two_ref, three_ref, ta_ref, *refs):
    outs = refs[-2 * SIDE :]
    z, core = place_ref[0], place_ref[1]
    slabs = (own_ref, one_ref, two_ref, three_ref)

    def pick(chip, first):
        back = (z - chip + SIDE) % SIDE
        value = slabs[0][pl.ds(first, 8), :]
        for s in range(1, SIDE):
            value = jnp.where(back == s, slabs[s][pl.ds(first, 8), :], value)
        return value

    tiles = []
    for row in range(STEPS):
        other = jnp.where(core == row % 2, 0, 1)
        for step in range(row):
            tiles.append(pick(row // 2, aligned(other * (STEPS * WIDTH) + step * WIDTH, 8)))
    for chip in range(SIDE):
        tiles.append(pick(chip, 2 * STEPS * WIDTH))
    for half in range(2):
        for by in range(SIDE):
            out = outs[half * SIDE + by]
            for tile in range(TILES // 2):
                out[tile] = tiles[half * (TILES // 2) + tile]
            quarter = (place_ref[2 + half] + by) % SIDE
            for tile in range(QTILES):
                first = aligned(FIRST[half] + quarter * QUARTER + tile * NB, NB)
                value = ta_ref[:, pl.ds(first, NB)]
                if half == 1 and tile == 0:
                    value = jnp.where(quarter == 0, 0.0, value)
                out[TILES // 2 + tile] = value


def hold_kernel(*refs):
    ins, outs, sems = refs[:4], refs[-5:-1], refs[-1]
    copies = [pltpu.make_async_copy(ins[i], outs[i], sems.at[i]) for i in range(4)]
    for copy in copies:
        copy.start()
    for copy in copies:
        copy.wait()


def line_kernel(*refs):
    for half in range(2):
        for by in range(SIDE):
            refs[-2 + half][by] = refs[half * SIDE + by][...]


def repack_kernel(*refs):
    first, second, (blocks, ta_first, ta_second) = refs[:4], refs[4:8], refs[-3:]
    for dy in range(SIDE):
        for dx in range(SIDE):
            at = dy * SIDE + dx
            for half, (source, ta) in enumerate(((first[dx].at[dy], ta_first), (second[dy].at[dx], ta_second))):
                for tile in range(TILES // 2):
                    blocks[half * (TILES // 2) + tile, at] = source[tile]
                for tile in range(QTILES):
                    ta[at * 8 : at * 8 + 8, tile * NB : (tile + 1) * NB] = source[TILES // 2 + tile]


def either(core, which, mine_ref, other_ref, tile):
    return jnp.where(core == which, mine_ref[tile], other_ref[tile]).reshape(NB, NB)


def block_of(core, mine_ref, other_ref, row, step, part):
    return either(core, part, mine_ref, other_ref, row * (row - 1) // 2 + step)


def near_inverse(place_ref, d_ref, part, step):
    y, x = place_ref[2], place_ref[3]
    rows = []
    for dy in range(SIDE):
        for dx in range(SIDE):
            col = ((y - dy + SIDE) % SIDE) * SIDE + (x - dx + SIDE) % SIDE
            rows.append(d_ref[part, step, pl.ds(aligned(col * 8, 8), 8), :])
    return jnp.concatenate(rows, axis=0)


def store_parts(ref, step, value):
    for part in range(2):
        ref[part, :, step * NB : (step + 1) * NB] = value[part * PER_COL : (part + 1) * PER_COL]


def forward_kernel(place_ref, mine_ref, other_ref, d_ref, *refs):
    first_ref, second_ref, sol_ref, acc, own = refs[-5:]
    core = place_ref[1]
    for row in range(STEPS):
        acc[row] = either(core, row % 2, mine_ref, other_ref, 28 + row // 2)
    lane = lax.broadcasted_iota(jnp.int32, (NB, NB), 1)
    for step in range(STEPS):
        a = acc[step]
        left = split(jnp.concatenate([a, times_i(a)], axis=1))
        near = jnp.concatenate([near_inverse(place_ref, d_ref, part, step) for part in range(2)], axis=1)
        x = dot_split(dot_nt, left, split(near))
        ix = times_i(x)
        natural = jnp.concatenate([d_ref[0, step], d_ref[1, step]], axis=1)
        own_left = split(jnp.concatenate([a[:8], times_i(a[:8])], axis=1))
        store_parts(sol_ref, step, dot_split(dot_nt, own_left, split(natural)))
        left = split(jnp.concatenate([x, ix], axis=1))
        for row in range(step + 1, STEPS):
            right = jnp.concatenate([block_of(core, mine_ref, other_ref, row, step, part) for part in range(2)], axis=0)
            acc[row] -= dot_split(dot_nn, left, split(right))
        for half, apart in enumerate((SIDE * WIDTH, WIDTH)):
            for by in range(SIDE):
                at = half * SIDE + by
                mine = own[at] if step else jnp.zeros((NB, NB), F32)
                for part, value in enumerate((x, ix)):
                    to = part * STEPS + step
                    moved = pltpu.roll(value, (to * WIDTH - by * apart) % NB, 1)
                    mine = jnp.where(lane // WIDTH == to, moved, mine)
                own[at] = mine
    for by in range(SIDE):
        second_ref[:, by * NB : (by + 1) * NB] = own[SIDE + by]
        for dy in range(SIDE):
            for dx in range(SIDE):
                from_row, to_row = (dy * SIDE + dx) * 8, (dx * SIDE + dy) * 8
                first_ref[to_row : to_row + 8, by * NB : (by + 1) * NB] = own[by, from_row : from_row + 8]


def backward_kernel(place_ref, loads_ref, *refs):
    sums, (mine_ref, other_ref, d_ref, out_ref, acc) = refs[:4], refs[4:]
    core = place_ref[1]
    acc[...] = jnp.zeros_like(acc)
    for step in reversed(range(STEPS)):
        v = loads_ref[:, step * NB : (step + 1) * NB]
        v -= (sums[0][step] + sums[1][step]) + (sums[2][step] + sums[3][step])
        right = jnp.concatenate([d_ref[0, step], -d_ref[1, step]], axis=0)
        y = dot_split(dot_nn, split(jnp.concatenate([v, times_i(v)], axis=1)), split(right))
        if step < STEPS - 1:
            u = acc[step]
            near = [near_inverse(place_ref, d_ref, part, step) for part in range(2)]
            right = split(jnp.concatenate([near[0], -near[1]], axis=0))
            y -= dot_split(dot_nn, split(jnp.concatenate([u, times_i(u)], axis=1)), right)
        store_parts(out_ref, step, y)
        left = split(jnp.concatenate([y, times_i(y)], axis=1))
        for other in range(step):
            right = [block_of(core, mine_ref, other_ref, step, other, part) for part in range(2)]
            acc[other] += dot_split(dot_nt, left, split(jnp.concatenate([right[0], -right[1]], axis=1)))


def trail_term(x_ref, by, piece_ref):
    return dot_split(dot_nn, split(x_ref[:, by * NB : (by + 1) * NB]), split(piece_ref[...]))


def zsum_term(place_ref, ta, half, by, piece_ref, out):
    q = dot_split(dot_nt, ta, split(piece_ref[...]))
    q = q - times_i(pltpu.roll(q, 64, 1))
    index = (place_ref[2 + half] - by + SIDE) % SIDE
    for dy in range(SIDE):
        out[dy, index, :, half * 64 : half * 64 + 64] = q[dy * 32 : dy * 32 + 32, :64]


def early_kernel(place_ref, *refs):
    zout, touts = refs[-3], refs[-2:]
    for half in range(2):
        ta = split(refs[2 + half][...])
        total = None
        for i, by in enumerate((0, 1, 3)):
            piece = refs[4 + half * 3 + i]
            zsum_term(place_ref, ta, half, by, piece, zout)
            term = trail_term(refs[half], by, piece)
            total = term if total is None else total + term
        touts[half][...] = total


def late_kernel(place_ref, *refs):
    zin, tins, pieces, outs = refs[4], refs[5:7], refs[7:9], refs[-2 * SIDE - 1 : -1]
    zsums = refs[-1]
    zsums[...] = zin[...]
    for half in range(2):
        zsum_term(place_ref, split(refs[2 + half][...]), half, 2, pieces[half], zsums)
        total = tins[half][...] + trail_term(refs[half], 2, pieces[half])
        for by in range(SIDE):
            outs[half * SIDE + by][:, :QUARTER] = -total[by * 32 : by * 32 + 32]
    for dy in range(SIDE):
        for index in range(SIDE):
            outs[SIDE + dy][:, QUARTER + index * NB : QUARTER + (index + 1) * NB] = zsums[dy, index]


def middle_kernel(*refs):
    got, outs = (refs[:SIDE], refs[SIDE : 2 * SIDE]), refs[-2 * SIDE :]
    for by in range(SIDE):
        rows = slice(by * 8, by * 8 + 8)
        for half in range(2):
            values = [ref[rows, :QUARTER] for ref in got[half]]
            outs[half * SIDE + by][:, :QUARTER] = (values[0] + values[1]) + (values[2] + values[3])
        for col in range(SIDE):
            values = [ref[rows, QUARTER + col * NB : QUARTER + (col + 1) * NB] for ref in got[1]]
            values.append((values[0] + values[1]) + (values[2] + values[3]))
            for dy in range(SIDE + 1):
                to = QUARTER + (dy * SIDE + col) * NB
                outs[SIDE + by][:, to : to + NB] = values[dy]


def last_kernel(place_ref, *refs):
    got, (out_ref, held) = refs[:SIDE], refs[-2:]
    for dy in range(SIDE):
        for col in range(SIDE):
            at = QUARTER + (dy * SIDE + col) * NB
            values = [ref[:, at : at + NB] for ref in got]
            value = (values[0] + values[1]) + (values[2] + values[3])
            held[(place_ref[2] + dy) % SIDE * SIDE + col] = pltpu.roll(value, 64, 1)
    for dx in range(SIDE):
        for y in range(SIDE):
            at = QUARTER + (SIDE * SIDE + y) * NB
            held[y * SIDE + (place_ref[3] + dx) % SIDE] += got[dx][:, at : at + NB]
    lane = lax.broadcasted_iota(jnp.int32, (8, NB), 1)
    for step in range(STEPS):
        value = jnp.zeros((8, NB), F32)
        for col in range(COLS_AXIS):
            moved = pltpu.roll(held[col], ((col - step) * WIDTH) % NB, 1)
            value = jnp.where(lane // WIDTH == col, moved, value)
        out_ref[step] = value


def finish_kernel(place_ref, loads_ref, *refs):
    pieces, out_ref = refs[: 2 * SIDE], refs[-1]
    for half in range(2):
        for by in range(SIDE):
            quarter = (place_ref[2 + half] + by) % SIDE
            to = aligned(FIRST[half] + quarter * QUARTER, NB)
            value = pieces[half * SIDE + by][:, :QUARTER]
            for part in range(2):
                rows = value[part * PER_COL : (part + 1) * PER_COL]
                loads = loads_ref[part, :, pl.ds(aligned(to + NB, NB), QUARTER)]
                out_ref[part, :, pl.ds(to, QUARTER)] = rows + loads


VMEM = pl.BlockSpec(memory_space=pltpu.VMEM)
SMEM = pl.BlockSpec(memory_space=pltpu.SMEM)
ANY = pl.BlockSpec(memory_space=pl.ANY)


def call(kernel, name, shapes, args, scratch=(), after=(), far=(), us=1):
    specs = [SMEM if arg.dtype == jnp.int32 else VMEM for arg in args]
    specs = [ANY if i in far else spec for i, spec in enumerate(specs)] + [ANY] * len(after)
    args = [*args, *after]
    return pl.pallas_call(
        kernel,
        out_shape=[jax.ShapeDtypeStruct(shape, F32) for shape in shapes],
        in_specs=specs,
        out_specs=[VMEM] * len(shapes),
        scratch_shapes=list(scratch),
        compiler_params=pltpu.CompilerParams(vmem_limit_bytes=LIMIT),
        cost_estimate=pl.CostEstimate(flops=0, bytes_accessed=3_500_000 * us, transcendentals=0),
        name=name,
    )(*args)


def to_other_core(array):
    return lax.ppermute(array, "row", [(r, r ^ 1) for r in range(ROWS_AXIS)])


def up_z(array, by):
    return lax.ppermute(array, "row", [(r, (r + 2 * by) % ROWS_AXIS) for r in range(ROWS_AXIS)])


def up(array, axis, by):
    def moved(c):
        y, x = c // SIDE, c % SIDE
        return ((y + by) % SIDE) * SIDE + x if axis == "y" else y * SIDE + (x + by) % SIDE

    return lax.ppermute(array, "col", [(c, moved(c)) for c in range(COLS_AXIS)])


def to_all(pieces, axis, sign=1):
    return [pieces[0]] + [up(pieces[by], axis, sign * by) for by in (1, 2, 3)]


AXES = (("y", "x"), ("x", "y"))


def cut(place, factor, distances, after=()):
    return call(
        functools.partial(cut_kernel, distances),
        "cut",
        [(NB, QUARTER)] * 2 * len(distances),
        [place, factor],
        [pltpu.SemaphoreType.DMA((2 * len(distances),))],
        after,
        (1,),
    )


def quarter_of(factor, place, half, by):
    return lax.dynamic_slice(factor, (0, NB + FIRST[half] + (place[2 + half] + by) % SIDE * QUARTER), (NB, QUARTER))


def body(load_vectors, panel_factor, diag_inverse, trail_adjoint, adjoint_loads):
    col, row = lax.axis_index("col"), lax.axis_index("row")
    place = jnp.stack([row // 2, row % 2, col // SIDE, col % SIDE]).astype(jnp.int32)
    core = row % 2
    factor = panel_factor.reshape(NB, LOCAL)
    parts = factor[:, :NB].reshape(2, STEPS * WIDTH, NB)
    keep = lax.dynamic_index_in_dim(parts, core, 0, False)
    got = to_other_core(lax.dynamic_index_in_dim(parts, 1 - core, 0, False))
    slab = jnp.concatenate([keep, got, load_vectors[:, :, :NB].reshape(8, NB)], axis=0)
    slabs = [slab] + [up_z(slab, by) for by in (1, 2, 3)]
    early = [quarter_of(factor, place, half, by) for half in range(2) for by in (1, 3)]
    one = [up(early[2 * half], AXES[half][0], 1) for half in range(2)]
    three = [up(early[2 * half + 1], AXES[half][0], 3) for half in range(2)]
    messages = call(
        pack_kernel,
        "pack",
        [(MESSAGE, 8, NB)] * 8,
        [place, *slabs, trail_adjoint.reshape(8, TRAIL_LOCAL)],
        after=one,
    )
    heard = [to_all(messages[half * SIDE : half * SIDE + SIDE], AXES[half][0]) for half in range(2)]
    first_lines = call(line_kernel, "line", [(SIDE, MESSAGE, 8, NB)] * 2, heard[0] + heard[1], after=three)
    lines = to_all([first_lines[0]] * SIDE, AXES[0][1]) + to_all([first_lines[1]] * SIDE, AXES[1][1])
    late = cut(place, factor, (0, 2), [lines[1], lines[5]])
    two = [up(late[2 * half + 1], AXES[half][0], 2) for half in range(2)]
    pieces = [[late[2 * half], one[half], two[half], three[half]] for half in range(2)]
    blocks, ta_first, ta_second = call(
        repack_kernel, "repack", [(TILES, COLS_AXIS, 8, NB)] + [(NB, QUARTER)] * 2, lines
    )
    window = (blocks, to_other_core(blocks))
    *trail_x, sol = call(
        forward_kernel,
        "forward",
        [(NB, SIDE * NB)] * 2 + [(2, PER_COL, STEPS * NB)],
        [place, *window, diag_inverse],
        [pltpu.VMEM((STEPS, NB, NB), F32)] * 2,
        us=6,
    )
    zpart, *tparts = call(
        early_kernel,
        "early",
        [(SIDE, SIDE, 32, NB)] + [(NB, QUARTER)] * 2,
        [place, *trail_x, ta_first, ta_second] + [pieces[half][by] for half in range(2) for by in (0, 1, 3)],
        us=6,
    )
    sent = call(
        late_kernel,
        "late",
        [(32, QUARTER)] * SIDE + [(32, QUARTER + SIDE * NB)] * SIDE,
        [place, *trail_x, ta_first, ta_second, zpart, *tparts, pieces[0][2], pieces[1][2]],
        [pltpu.VMEM((SIDE, SIDE, 32, NB), F32)],
        us=3,
    )
    mine = lax.dynamic_slice_in_dim(adjoint_loads, col * PER_COL, PER_COL, 1).reshape(8, STEPS * NB)
    held = call(
        hold_kernel,
        "hold",
        [window[0].shape, window[1].shape, diag_inverse.shape, mine.shape],
        [*window, diag_inverse, mine],
        [pltpu.SemaphoreType.DMA((4,))],
        sent[:1],
        range(4),
    )
    met = [to_all(sent[half * SIDE : half * SIDE + SIDE], AXES[half][1], -1) for half in range(2)]
    sent = call(
        middle_kernel,
        "middle",
        [(8, QUARTER)] * SIDE + [(8, QUARTER + 20 * NB)] * SIDE,
        met[0] + met[1],
        after=held[:1],
    )
    met = [to_all(sent[half * SIDE : half * SIDE + SIDE], AXES[half][0], -1) for half in range(2)]
    (zown,) = call(
        last_kernel, "last", [(STEPS, 8, NB)], [place, *met[1]], [pltpu.VMEM((COLS_AXIS, 8, NB), F32)]
    )
    zchip = zown + to_other_core(zown)
    zsums = [zchip] + [up_z(zchip, by) for by in (1, 2, 3)]
    (adj,) = call(
        backward_kernel,
        "backward",
        [(2, PER_COL, STEPS * NB)],
        [place, held[3], *zsums, *held[:3]],
        [pltpu.VMEM((STEPS, 8, NB), F32)],
        us=6,
    )
    (residual,) = call(
        finish_kernel,
        "finish",
        [(2, PER_COL, TRAIL_LOCAL)],
        [place, load_vectors, *met[0], *met[1]],
        after=[zown],
    )
    return sol, residual, adj


def solution(mesh):
    in_specs = (
        P(None, "col", "row"),
        P(None, "col", None, None, "row"),
        P(),
        P(None, "col", "row"),
        P(),
    )
    out_specs = (P(None, "col", None), P(None, "col", "row"), P(None, "col", None))
    return jax.shard_map(body, mesh=mesh, in_specs=in_specs, out_specs=out_specs, check_vma=False)
```
